256 devices in a mesh: tm: 16 (over z_hi, x), space: 16 (over z_lo, y, core).
Axes of the slice: x: 4, y: 4, z: 8 (z_hi: 4, z_lo: 2; z = z_hi * 2 + z_lo), core: 2. Of those that a mesh axis runs over, the one named last changes fastest.
Arguments:
- forcing: float32 [16, 32, 128, 256], P('tm', 'space'), may hold values from -4 to 4
- iterate: float32 [16, 32, 128, 256], P('tm', 'space'), may hold values from -4 to 4
- kappa: float32 [32, 128, 256], P('space'), may hold values from 0.5 to 2
- velocity: float32 [3, 32, 128, 256], P(None, 'space'), may hold values from -1 to 1
Outputs:
- updated: float32 [16, 32, 128, 256], P('tm', 'space')
The draws below stay inside these ranges and needn't reach their ends.
All inputs are finite; a program needn't handle non-finite values.
Results may differ from the reference program's by a relative error of at most 0.0003.
Values sent between devices are 32-bit elements; how exact they have to be, the bound alone decides.
No kernel may reach another device: no remote copies, remote signals or barrier semaphores. Data moves between devices by JAX's collectives and lax.ppermute only.
A program may use at most 64 MiB of HBM per device.

```python
import math
import jax
import jax.numpy as jnp
from jax import lax

NY = 128
NX = 256
SWEEPS = 8
WINDOW = 16
NZ = 32


def draw_forcing(key, part):
    key = jax.random.fold_in(key, 11)
    shape = (WINDOW, NZ, NY, NX)
    return jnp.clip(jax.random.normal(key, shape, jnp.float32), -4.0, 4.0)


def block_levels(rng, dims, cuts, least, largest):
    level, own = 1.0, jax.random.fold_in(rng, 6)
    for dim, shards_of in cuts:
        draws = jnp.exp(jax.random.uniform(jax.random.fold_in(own, dim), (shards_of,), jnp.float32, least / len(cuts), largest / len(cuts)))
        level = level * jnp.repeat(draws, dims[dim] // shards_of).reshape([-1 if axis == dim else 1 for axis in range(len(dims))])
    return level


def normal_values(stream_key, extent, scale, limit, cuts=(), dtype=jnp.bfloat16):
    values = jax.random.normal(stream_key, extent, jnp.float32) * scale
    if len(cuts) > 0:
        values = block_levels(stream_key, extent, cuts, -0.22, 0.18) * values
    return jnp.clip(values, min=-limit, max=limit).astype(dtype)


def setup_inputs(seed: int = 0) -> dict:
    key_of = jax.random.split(jax.random.key(seed), 5)
    return {
        "forcing": draw_forcing(jax.random.fold_in(key_of[4], 71), 0),
        "iterate": normal_values(key_of[1], (WINDOW, NZ, NY, NX), 1.0, 4.0, ((0, 16), (1, 16)), jnp.float32),
        "kappa": jnp.clip(jnp.exp(math.log(2.0) - 1.3862944 * jax.random.uniform(key_of[2], (NZ, NY, NX), jnp.float32) ** block_levels(key_of[2], (NZ, NY, NX), ((0, 16),), -0.2, 0.2)), 0.5, 2.0),
        "velocity": jnp.clip(jax.random.uniform(key_of[3], (3, NZ, NY, NX), jnp.float32, -1.0, 1.0) * block_levels(key_of[3], (3, NZ, NY, NX), ((1, 16),), -0.4, 0.0), -1.0, 1.0),
    }


ALPHA = 0.05
TIME_STEP = 0.5


def coefficients(kappa_rim, velocity):
    padded = jnp.pad(kappa_rim, ((0, 0), (1, 1), (1, 1)))
    centre = padded[1:-1, 1:-1, 1:-1]
    plus_z = 0.5 * (centre + padded[2:, 1:-1, 1:-1])
    minus_z = 0.5 * (centre + padded[:-2, 1:-1, 1:-1])
    plus_y = 0.5 * (centre + padded[1:-1, 2:, 1:-1])
    minus_y = 0.5 * (centre + padded[1:-1, :-2, 1:-1])
    plus_x = 0.5 * (centre + padded[1:-1, 1:-1, 2:])
    minus_x = 0.5 * (centre + padded[1:-1, 1:-1, :-2])
    diagonal = plus_z + minus_z + plus_y + minus_y + plus_x + minus_x
    half_velocity = 0.5 * velocity
    coeffs = (plus_z - half_velocity[0], minus_z + half_velocity[0],
              plus_y - half_velocity[1], minus_y + half_velocity[1],
              plus_x - half_velocity[2], minus_x + half_velocity[2])
    return coeffs, diagonal


def neighbour_sum(coeffs, field_rim):
    lead = [(0, 0)] * (field_rim.ndim - 3)
    padded = jnp.pad(field_rim, lead + [(0, 0), (1, 1), (1, 1)])
    total = coeffs[0] * padded[..., 2:, 1:-1, 1:-1] + coeffs[1] * padded[..., :-2, 1:-1, 1:-1]
    total = total + coeffs[2] * padded[..., 1:-1, 2:, 1:-1] + coeffs[3] * padded[..., 1:-1, :-2, 1:-1]
    total = total + coeffs[4] * padded[..., 1:-1, 1:-1, 2:] + coeffs[5] * padded[..., 1:-1, 1:-1, :-2]
    return total


def jacobi(coeffs, diagonal, spectrum, frequency, window, halo_fn):
    decay = jnp.exp(jnp.log(jnp.float32(ALPHA)) / window)
    phase_angle = 2.0 * math.pi * frequency / window
    sigma_real = (1.0 - decay * jnp.cos(phase_angle)) / TIME_STEP
    sigma_imag = decay * jnp.sin(phase_angle) / TIME_STEP
    denom_real = sigma_real + diagonal
    scale_inv = 1.0 / (denom_real * denom_real + sigma_imag * sigma_imag)
    inverse_real = denom_real * scale_inv
    inverse_imag = -sigma_imag * scale_inv

    def divide(values):
        return jnp.stack([values[0] * inverse_real - values[1] * inverse_imag,
                          values[0] * inverse_imag + values[1] * inverse_real])

    solved = divide(spectrum)
    for repeat in range(SWEEPS - 1):
        solved = divide(spectrum + neighbour_sum(coeffs, halo_fn(solved)))
    return solved


def reference(forcing, iterate, kappa, velocity):
    window = forcing.shape[0]
    coeffs, diagonal = coefficients(jnp.pad(kappa, ((1, 1), (0, 0), (0, 0))), velocity)

    def apply_one(current):
        return diagonal * current - neighbour_sum(coeffs, jnp.pad(current, ((1, 1), (0, 0), (0, 0))))

    applied = lax.map(apply_one, iterate)
    previous = jnp.concatenate([jnp.zeros_like(iterate[:1]), iterate[:-1]], 0)
    resid = forcing - (iterate - previous) / TIME_STEP - applied
    counter = jnp.arange(window).astype(jnp.float32)
    growth = jnp.exp(counter / window * jnp.log(jnp.float32(ALPHA)))
    scaled = resid * growth[:, None, None, None]
    transformed = jnp.fft.fft(scaled, axis=0)
    spectrum = jnp.stack([jnp.real(transformed), jnp.imag(transformed)], 1).astype(jnp.float32)

    def pad_planes(values):
        return jnp.pad(values, ((0, 0), (1, 1), (0, 0), (0, 0)))

    def solve_one(record):
        return jacobi(coeffs, diagonal, record[0], record[1], window, pad_planes)

    solved = lax.map(solve_one, (spectrum, counter))
    back = jnp.fft.ifft(solved[:, 0] + 1j * solved[:, 1], axis=0)
    correction = jnp.real(back).astype(jnp.float32)
    return iterate + correction / growth[:, None, None, None]
```

```python
import functools
import math

import jax
import jax.numpy as jnp
import numpy as np
from jax import lax
from jax.experimental import pallas as pl
from jax.experimental.pallas import tpu as pltpu
from jax.sharding import PartitionSpec as P

SWEEPS = 8
ALPHA = 0.05
TIME_STEP = 0.5
WINDOW = 16
DECAY = ALPHA ** (1.0 / WINDOW)
NZ, NY, NX = 32, 128, 256
OWN = NX // WINDOW
WIDE = OWN + 16
HALF = OWN // 2
HWIDE = HALF + 16


def time_tables():
    n = np.arange(WINDOW)
    ahead = np.zeros((WINDOW, WINDOW))
    back = np.zeros((WINDOW, WINDOW))
    for p in range(8):
        angle = 2.0 * np.pi * p * n / WINDOW
        ahead[p] = np.cos(angle)
        ahead[8 + p] = -np.sin(angle) if p else np.cos(np.pi * n)
        back[:, p] = np.cos(angle) * (2.0 if p else 1.0)
        back[:, 8 + p] = -2.0 * np.sin(angle) if p else np.cos(np.pi * n)
    ahead = ahead * DECAY**n[None, :]
    back = back / WINDOW * DECAY ** -n[:, None].astype(float)
    return ahead.astype(np.float32), back.astype(np.float32)


def shift_table():
    rows = []
    for s in range(16):
        p = s % 8
        angle = 2.0 * np.pi * p / WINDOW
        real = (1.0 - DECAY * np.cos(angle)) / TIME_STEP
        imag = DECAY * np.sin(angle) / TIME_STEP
        other = real if p else (1.0 + DECAY) / TIME_STEP
        rows.append([real, other, imag if p else 0.0])
    return np.asarray(rows, np.float32)


def swapped(block, axis, pairs):
    return lax.ppermute(block, axis, pairs)


def coefficients(kappa_rim, velocity):
    padded = jnp.pad(kappa_rim, ((0, 0), (1, 1), (1, 1)))
    centre = padded[1:-1, 1:-1, 1:-1]
    plus_z = 0.5 * (centre + padded[2:, 1:-1, 1:-1])
    minus_z = 0.5 * (centre + padded[:-2, 1:-1, 1:-1])
    plus_y = 0.5 * (centre + padded[1:-1, 2:, 1:-1])
    minus_y = 0.5 * (centre + padded[1:-1, :-2, 1:-1])
    plus_x = 0.5 * (centre + padded[1:-1, 1:-1, 2:])
    minus_x = 0.5 * (centre + padded[1:-1, 1:-1, :-2])
    diagonal = plus_z + minus_z + plus_y + minus_y + plus_x + minus_x
    half_velocity = 0.5 * velocity
    coeffs = (
        plus_z - half_velocity[0],
        minus_z + half_velocity[0],
        plus_y - half_velocity[1],
        minus_y + half_velocity[1],
        plus_x - half_velocity[2],
        minus_x + half_velocity[2],
    )
    return (coeffs, diagonal)


def neighbour_sum(coeffs, field_rim):
    padded = jnp.pad(field_rim, [(0, 0), (1, 1), (1, 1)])
    total = coeffs[0] * padded[2:, 1:-1, 1:-1] + coeffs[1] * padded[:-2, 1:-1, 1:-1]
    total = total + coeffs[2] * padded[1:-1, 2:, 1:-1] + coeffs[3] * padded[1:-1, :-2, 1:-1]
    total = total + coeffs[4] * padded[1:-1, 1:-1, 2:] + coeffs[5] * padded[1:-1, 1:-1, :-2]
    return total


def jacobi_kernel(where, shift, spec, fields, out, kap, cof, inv, field_a, field_b):
    first = pl.multiple_of(where[0], HALF)
    start = where[1]
    column = start + lax.broadcasted_iota(jnp.int32, (HWIDE, NY), 0)
    lane = lax.broadcasted_iota(jnp.int32, (HWIDE, NY), 1)
    real, other, imag = shift[0], shift[1], shift[2]
    zeros = jnp.zeros((HWIDE, NY), jnp.float32)
    kap[0] = zeros
    kap[NZ + 1] = zeros
    for buf in (field_a, field_b):
        for part in range(2):
            buf[0, part] = zeros
            buf[NZ + 1, part] = zeros

    def load_kappa(s, carry):
        for plane in range(2):
            kap[2 * s + plane + 1] = fields[s, 0, plane, pl.ds(first, HWIDE), :]
        return carry

    lax.fori_loop(0, NZ // 2, load_kappa, 0)

    def divide(z, total_real, total_imag):
        inv_real, inv_other, inv_imag = inv[z, 0], inv[z, 1], inv[z, 2]
        return (
            total_real * inv_real - total_imag * inv_imag,
            total_real * inv_imag + total_imag * inv_other,
        )

    def prepare(z, carry):
        centre = kap[z + 1]
        half = [
            0.5 * fields[z // 2, 1 + d, z % 2, pl.ds(first, HWIDE), :] for d in range(3)
        ]
        up_z = 0.5 * (centre + kap[z + 2])
        down_z = 0.5 * (centre + kap[z])
        up_y = 0.5 * (centre + jnp.where(lane < NY - 1, pltpu.roll(centre, NY - 1, 1), 0.0))
        down_y = 0.5 * (centre + jnp.where(lane > 0, pltpu.roll(centre, 1, 1), 0.0))
        up_x = 0.5 * (centre + pltpu.roll(centre, HWIDE - 1, 0))
        down_x = 0.5 * (centre + pltpu.roll(centre, 1, 0))
        diagonal = up_z + down_z + up_y + down_y + up_x + down_x
        cof[z, 0] = up_z - half[0]
        cof[z, 1] = down_z + half[0]
        cof[z, 2] = jnp.where(lane < NY - 1, up_y - half[1], 0.0)
        cof[z, 3] = jnp.where(lane > 0, down_y + half[1], 0.0)
        cof[z, 4] = jnp.where(column < NX - 1, up_x - half[2], 0.0)
        cof[z, 5] = jnp.where(column > 0, down_x + half[2], 0.0)
        den = real + diagonal
        den_other = other + diagonal
        scale = 1.0 / (den * den + imag * imag)
        inv[z, 0] = den * scale
        inv[z, 1] = den_other / (den_other * den_other + imag * imag)
        inv[z, 2] = -imag * scale
        new_real, new_imag = divide(z, spec[z, 0], spec[z, 1])
        field_a[z + 1, 0] = new_real
        field_a[z + 1, 1] = new_imag
        return carry

    lax.fori_loop(0, NZ, prepare, 0)

    def total_of(src, z, part):
        centre = src[z + 1, part]
        total = cof[z, 0] * src[z + 2, part] + cof[z, 1] * src[z, part]
        total += cof[z, 2] * pltpu.roll(centre, NY - 1, 1) + cof[z, 3] * pltpu.roll(centre, 1, 1)
        total += cof[z, 4] * pltpu.roll(centre, HWIDE - 1, 0) + cof[z, 5] * pltpu.roll(centre, 1, 0)
        return total + spec[z, part]

    def sweep(src, dst, last):
        def body(z, carry):
            new_real, new_imag = divide(z, total_of(src, z, 0), total_of(src, z, 1))
            if last:
                out[z, 0] = new_real[8 : 8 + HALF]
                out[z, 1] = new_imag[8 : 8 + HALF]
            else:
                dst[z + 1, 0] = new_real
                dst[z + 1, 1] = new_imag
            return carry

        lax.fori_loop(0, NZ, body, 0)

    buffers = (field_a, field_b)
    for repeat in range(SWEEPS - 1):
        sweep(buffers[repeat % 2], buffers[(repeat + 1) % 2], repeat == SWEEPS - 2)


def jacobi(where, shift, spec, fields):
    vmem = pl.BlockSpec(memory_space=pltpu.VMEM)
    smem = pl.BlockSpec(memory_space=pltpu.SMEM)
    return pl.pallas_call(
        jacobi_kernel,
        out_shape=jax.ShapeDtypeStruct((NZ, 2, HALF, NY), jnp.float32),
        in_specs=[smem, smem, vmem, vmem],
        out_specs=vmem,
        scratch_shapes=[
            pltpu.VMEM((NZ + 2, HWIDE, NY), jnp.float32),
            pltpu.VMEM((NZ, 6, HWIDE, NY), jnp.float32),
            pltpu.VMEM((NZ, 3, HWIDE, NY), jnp.float32),
            pltpu.VMEM((NZ + 2, 2, HWIDE, NY), jnp.float32),
            pltpu.VMEM((NZ + 2, 2, HWIDE, NY), jnp.float32),
        ],
        compiler_params=pltpu.CompilerParams(vmem_limit_bytes=32 * 1024 * 1024),
    )(where, shift, spec, fields)


def shards(forcing, iterate, kappa, velocity):
    step = lax.axis_index("tm")
    place = lax.axis_index("space")
    ahead, back = time_tables()
    current = iterate[0]
    both = jnp.stack([kappa, current])
    even = place % 2 == 0
    inner_send = jnp.where(even, both[:, 1], both[:, 0])
    outer_send = jnp.where(even, both[:, 0], both[:, 1])
    previous = lax.ppermute(current, "tm", [(i, i + 1) for i in range(WINDOW - 1)])
    inner = lax.ppermute(inner_send, "space", [(i, i ^ 1) for i in range(16)])
    pairs = [(i, i + 1) for i in range(1, 15, 2)] + [(i + 1, i) for i in range(1, 15, 2)]
    outer = lax.ppermute(outer_send, "space", pairs)
    low = jnp.where(even, outer, inner)
    high = jnp.where(even, inner, outer)
    rims = jnp.concatenate([low[:, None], both, high[:, None]], axis=1)

    fields = jnp.pad(jnp.concatenate([kappa[None], velocity]), ((0, 0), (0, 0), (0, 0), (8, 8)))
    fields = lax.dynamic_slice_in_dim(fields, step * OWN, WIDE, 3)
    fields = lax.all_gather(fields.transpose(0, 1, 3, 2), "space")

    coeffs, diagonal = coefficients(rims[0], velocity)
    applied = diagonal * current - neighbour_sum(coeffs, rims[1])
    resid = forcing[0] - (current - previous) / TIME_STEP - applied
    turned = jnp.pad(resid.transpose(0, 2, 1), ((0, 0), (8, 8), (0, 0)))
    sent = jnp.stack([turned[:, OWN * c : OWN * c + WIDE] for c in range(WINDOW)])
    times = lax.all_to_all(sent, "tm", 0, 0)
    spectrum = jnp.einsum("cn,nzxy->czxy", ahead, times, precision="highest")
    parts = spectrum.reshape(2, 8, 2, WIDE, NY).transpose(1, 2, 0, 3, 4)
    sent = jnp.concatenate([parts[:, :, :, :HWIDE], parts[:, :, :, HALF : HALF + HWIDE]])
    spec = lax.all_to_all(sent, "space", 0, 0).reshape(NZ, 2, HWIDE, NY)
    first = place // 8 * HALF
    where = jnp.stack([first, step * OWN - 8 + first]).astype(jnp.int32)
    shift = jnp.asarray(shift_table())[place]
    solved = jacobi(where, shift, spec, fields)
    solved = lax.all_to_all(solved.reshape(16, 2, 2, HALF, NY), "space", 0, 0)
    solved = solved.reshape(2, 8, 2, 2, HALF, NY).transpose(3, 1, 2, 0, 4, 5)
    solved = solved.reshape(WINDOW, 2, OWN, NY)
    correction = jnp.einsum("nc,czxy->nzxy", back, solved, precision="highest")
    correction = lax.all_to_all(correction, "tm", 0, 0)
    correction = correction.transpose(1, 3, 0, 2).reshape(2, NY, NX)
    return (current + correction)[None]


def solution(mesh):
    in_specs = (
        P("tm", "space", None, None),
        P("tm", "space", None, None),
        P("space", None, None),
        P(None, "space", None, None),
    )
    out_specs = P("tm", "space", None, None)
    return jax.shard_map(shards, mesh=mesh, in_specs=in_specs, out_specs=out_specs, check_vma=False)
```

```python
import math

import jax
import jax.numpy as jnp
from jax import lax
from jax.experimental import pallas as pl
from jax.experimental.pallas import tpu as pltpu
from jax.sharding import PartitionSpec as P

SWEEPS = 8
ALPHA = 0.05
TIME_STEP = 0.5
WINDOW = 16
DECAY = ALPHA ** (1.0 / WINDOW)
NZ, NY, NX = 32, 128, 256
OWN = NX // WINDOW
WIDE = OWN + 16
SLAB = 2
CHIP = 4
CHIPS = NZ // CHIP
FIRST = 3
REACH = 10
NARROW = OWN + 8
REALS = 8


def time_scale(n):
    return DECAY**n


def shift_rows():
    rows = []
    for p in range(8):
        angle = 2.0 * math.pi * p / WINDOW
        real = (1.0 - DECAY * math.cos(angle)) / TIME_STEP
        imag = DECAY * math.sin(angle) / TIME_STEP
        other = real if p else (1.0 + DECAY) / TIME_STEP
        rows.append((real, other, imag if p else 0.0))
    return rows


def spectrum_of(times):
    even = [times[j] + times[j + 8] for j in range(8)]
    odd = [times[j] - times[j + 8] for j in range(8)]
    f = [even[j] + even[j + 4] for j in range(4)]
    g = [even[j] - even[j + 4] for j in range(4)]
    parts = [None] * 16
    parts[0] = (f[0] + f[2]) + (f[1] + f[3])
    parts[8] = (f[0] + f[2]) - (f[1] + f[3])
    parts[4] = f[0] - f[2]
    parts[12] = f[3] - f[1]
    root = math.sqrt(0.5)
    less, more = (g[1] - g[3]) * root, (g[1] + g[3]) * root
    parts[2] = g[0] + less
    parts[6] = g[0] - less
    parts[10] = -(g[2] + more)
    parts[14] = g[2] - more
    less = [odd[j] - odd[8 - j] for j in range(1, 4)]
    more = [odd[j] + odd[8 - j] for j in range(1, 4)]
    for k in (1, 3, 5, 7):
        angle = math.pi * k / 8
        parts[k] = odd[0] + sum(math.cos(angle * (j + 1)) * less[j] for j in range(3))
        tail = sum(math.sin(angle * (j + 1)) * more[j] for j in range(3))
        parts[8 + k] = -(tail + odd[4]) if k % 4 == 1 else odd[4] - tail
    return parts


def times_of(parts):
    plus, minus = parts[0] + parts[8], parts[0] - parts[8]
    two = [None if j in (0, 8) else 2.0 * parts[j] for j in range(16)]
    f = [plus + two[4], minus - two[12], plus - two[4], minus + two[12]]
    root = math.sqrt(0.5)
    g = [
        two[2] + two[6],
        root * ((two[2] - two[10]) - (two[6] + two[14])),
        two[14] - two[10],
        root * ((two[6] - two[14]) - (two[2] + two[10])),
    ]
    even = [f[j] + g[j] for j in range(4)] + [f[j] - g[j] for j in range(4)]
    odd = [None] * 8
    odd[0] = (two[1] + two[3]) + (two[5] + two[7])
    odd[4] = (two[11] + two[15]) - (two[9] + two[13])
    for n in range(1, 4):
        c = sum(math.cos(math.pi * p * n / 8) * two[p] for p in (1, 3, 5, 7))
        s = sum(math.sin(math.pi * p * n / 8) * two[8 + p] for p in (1, 3, 5, 7))
        odd[n] = c - s
        odd[8 - n] = -(c + s)
    return [even[n] + odd[n] for n in range(8)] + [even[n] - odd[n] for n in range(8)]


def entry_kernel(iterate, kappa, outer, inner, sems):
    parity = lax.axis_index("space") % 2
    copies = [
        pltpu.make_async_copy(iterate.at[0, parity], outer.at[0], sems.at[0]),
        pltpu.make_async_copy(kappa.at[parity], outer.at[1], sems.at[1]),
        pltpu.make_async_copy(iterate.at[0, 1 - parity], inner.at[0], sems.at[2]),
        pltpu.make_async_copy(kappa.at[1 - parity], inner.at[1], sems.at[3]),
    ]
    for copy in copies:
        copy.start()
    for copy in copies:
        copy.wait()


def fields_kernel(kappa, velocity, out, held, turned, sems):
    step = lax.axis_index("tm")
    copies = [pltpu.make_async_copy(kappa, held.at[0], sems.at[0])]
    copies += [pltpu.make_async_copy(velocity.at[d], held.at[1 + d], sems.at[1 + d]) for d in range(3)]
    for copy in copies:
        copy.start()
    edge = jnp.zeros((8, NY), jnp.float32)
    for field in range(4):
        copies[field].wait()
        for plane in range(2):
            spot = turned.at[2 * field + plane]
            spot[0:8] = edge
            spot[8 : 8 + NX] = held[field, plane].T
            spot[8 + NX : 16 + NX] = edge
            out[field, plane] = spot[pl.ds(pl.multiple_of(step * OWN, OWN), WIDE), :]


def inside_kernel(forcing, iterate, kappa, velocity, base, rim, value):
    row = lax.broadcasted_iota(jnp.int32, (NY, NX), 0)
    lane = lax.broadcasted_iota(jnp.int32, (NY, NX), 1)

    def shifted(array, dim, up):
        extent = NY if dim == 0 else NX
        index = row if dim == 0 else lane
        inside = index < extent - 1 if up else index > 0
        return jnp.where(inside, pltpu.roll(array, extent - 1 if up else 1, dim), 0.0)

    for plane in range(2):
        centre, here = kappa[plane], iterate[0, plane]
        towards = -1.0 if plane == 0 else 1.0
        half = 0.5 * velocity[0, plane]
        face = 0.5 * (centre + kappa[1 - plane])
        diagonal = face + 0.5 * centre
        total = (face + towards * half) * iterate[0, 1 - plane]
        rim[plane] = 0.5 * centre - towards * half
        for dim in range(2):
            half = 0.5 * velocity[1 + dim, plane]
            for up, sign in ((True, -1.0), (False, 1.0)):
                face = 0.5 * (centre + shifted(centre, dim, up))
                diagonal += face
                total += (face + sign * half) * shifted(here, dim, up)
        base[plane] = forcing[0, plane] - here * (1.0 / TIME_STEP) - (diagonal * here - total)
        value[plane] = here


def resid_kernel(base, rim, value, previous, outer, inner, out, turned):
    step = lax.axis_index("tm")
    place = lax.axis_index("space")
    even = place % 2 == 0
    growth = jnp.exp(jnp.full((1, 1), step.astype(jnp.float32) / WINDOW * math.log(ALPHA), jnp.float32))
    carried = jnp.where(step == 0, 0.0, 1.0 / TIME_STEP)
    edge = jnp.zeros((8, NY), jnp.float32)
    for plane in range(2):
        side, other = (outer, inner) if plane == 0 else (inner, outer)
        ends = place == 0 if plane == 0 else place == 2 * CHIPS - 1
        here = value[plane]
        near = jnp.where(ends, 0.0, jnp.where(even, side[0], other[0]))
        far = jnp.where(ends, 0.0, 0.5 * jnp.where(even, side[1], other[1]))
        resid = base[plane] + previous[0, plane] * carried + (rim[plane] + far) * near - far * here
        turned[plane, 0:8] = edge
        turned[plane, 8 : 8 + NX] = (resid * growth).T
        turned[plane, 8 + NX : 16 + NX] = edge
        for c in range(WINDOW):
            out[c, plane] = turned[plane, OWN * c : OWN * c + WIDE]


def ahead_kernel(times, fields, above, below, keep, send):
    core = lax.axis_index("space") % 2
    for plane in range(SLAB):
        for tile in range(WIDE // 8):
            rows = slice(8 * tile, 8 * tile + 8)
            parts = spectrum_of([times[n, plane, rows] for n in range(WINDOW)])
            for j in range(REALS):
                p, part = j % 4, j // 4
                low, high = parts[8 * part + p], parts[8 * part + 4 + p]
                keep[plane, j, rows] = jnp.where(core == 0, low, high)
                send[REALS * plane + j, rows] = jnp.where(core == 0, high, low)
    spot = SLAB * REALS
    for source in (below, fields, above):
        for field in range(4):
            for plane in range(SLAB):
                send[spot] = source[field, plane]
                spot += 1


def gather_kernel(keep, got, chip, up, down):
    core = lax.axis_index("space") % 2
    for j in range(REALS):
        for plane in range(CHIP):
            mine, theirs = keep[plane % SLAB, j], got[REALS * (plane % SLAB) + j]
            value = jnp.where(core == plane // SLAB, mine, theirs)
            chip[plane, j] = value
            if plane >= CHIP - FIRST:
                up[plane - (CHIP - FIRST), j] = value
            if plane < FIRST:
                down[plane, j] = value


def back_kernel(mine, theirs, out):
    core = lax.axis_index("space") % 2
    for plane in range(SLAB):
        for tile in range(OWN // 8):
            rows = slice(8 * tile, 8 * tile + 8)
            parts = [None] * 16
            for j in range(REALS):
                p, part = j % 4, j // 4
                one, two = mine[plane, j, rows], theirs[plane, j, rows]
                parts[8 * part + p] = jnp.where(core == 0, one, two)
                parts[8 * part + 4 + p] = jnp.where(core == 0, two, one)
            values = times_of(parts)
            for n in range(WINDOW):
                out[n, plane, rows] = values[n] * (time_scale(-n) / WINDOW)


def update_kernel(correction, iterate, out):
    for plane in range(SLAB):
        turned = correction[:, plane].reshape(NX, NY).T
        out[0, plane] = iterate[0, plane] + turned


def prepare_kernel(fields, above, below, got, cof, held):
    place = lax.axis_index("space")
    core, chip = place % 2, place // 2
    start = lax.axis_index("tm") * OWN - 8
    column = start + lax.broadcasted_iota(jnp.int32, (WIDE, NY), 0)
    lane = lax.broadcasted_iota(jnp.int32, (WIDE, NY), 1)
    rows = shift_rows()
    shifts = [[jnp.where(core == 0, rows[j][i], rows[4 + j][i]) for i in range(3)] for j in range(4)]
    spot = SLAB * REALS
    for third, source in enumerate((below, fields, above)):
        for field in range(4):
            for plane in range(SLAB):
                value, other = source[field, plane], got[spot]
                spot += 1
                if field == 0 and third != 1:
                    outside = chip == (0 if third == 0 else CHIPS - 1)
                    value, other = jnp.where(outside, 0.0, value), jnp.where(outside, 0.0, other)
                held[field, CHIP * third + plane] = jnp.where(core == 0, value, other)
                held[field, CHIP * third + SLAB + plane] = jnp.where(core == 0, other, value)
    for z in range(REACH):
        spot = z + 1
        centre = held[0, spot]
        half = [0.5 * held[1 + d, spot] for d in range(3)]
        up_z = 0.5 * (centre + held[0, spot + 1])
        down_z = 0.5 * (centre + held[0, spot - 1])
        up_y = 0.5 * (centre + jnp.where(lane < NY - 1, pltpu.roll(centre, NY - 1, 1), 0.0))
        down_y = 0.5 * (centre + jnp.where(lane > 0, pltpu.roll(centre, 1, 1), 0.0))
        up_x = 0.5 * (centre + pltpu.roll(centre, WIDE - 1, 0))
        down_x = 0.5 * (centre + pltpu.roll(centre, 1, 0))
        diagonal = up_z + down_z + up_y + down_y + up_x + down_x
        plus_z, minus_z = up_z - half[0], down_z + half[0]
        if spot == 2 * CHIP - 1:
            plus_z = jnp.where(chip == CHIPS - 1, 0.0, plus_z)
        if spot == CHIP:
            minus_z = jnp.where(chip == 0, 0.0, minus_z)
        cof[z, 0] = plus_z
        cof[z, 1] = minus_z
        cof[z, 2] = jnp.where(lane < NY - 1, up_y - half[1], 0.0)
        cof[z, 3] = jnp.where(lane > 0, down_y + half[1], 0.0)
        cof[z, 4] = jnp.where(column < NX - 1, up_x - half[2], 0.0)
        cof[z, 5] = jnp.where(column > 0, down_x + half[2], 0.0)
        for j, (real, other, imag) in enumerate(shifts):
            den = real + diagonal
            scale = 1.0 / (den * den + imag * imag)
            cof[z, 6 + 2 * j] = den * scale
            cof[z, 7 + 2 * j] = -imag * scale
            if j == 0:
                den = other + diagonal
                cof[z, 14] = den / (den * den + imag * imag)


def divide(cof, z, j, total_real, total_imag):
    inv_real, inv_imag = cof[z, 6 + 2 * j], cof[z, 7 + 2 * j]
    inv_other = cof[z, 14] if j == 0 else inv_real
    return (
        total_real * inv_real - total_imag * inv_imag,
        total_real * inv_imag + total_imag * inv_other,
    )


def part_of(field, z, r, ahead=0):
    start = 8 + WIDE * (REALS * z + r) + ahead
    return field.at[start : start + WIDE]


def sweeps(cof, spec_of, src, dst, planes, shift, finish):
    for number, (first, end) in enumerate(planes):
        for z in range(first, end):
            here = z + shift
            for j in range(4):
                totals = []
                for r in (j, 4 + j):
                    centre = part_of(src, here, r)[...]
                    total = cof[z, 0] * part_of(src, here + 1, r)[...] + cof[z, 1] * part_of(src, here - 1, r)[...]
                    total += cof[z, 2] * pltpu.roll(centre, NY - 1, 1) + cof[z, 3] * pltpu.roll(centre, 1, 1)
                    total += cof[z, 4] * part_of(src, here, r, 1)[...] + cof[z, 5] * part_of(src, here, r, -1)[...]
                    totals.append(total + spec_of(z, r))
                for r, value in zip((j, 4 + j), divide(cof, z, j, *totals)):
                    if number == len(planes) - 1:
                        finish(z, r, value)
                    else:
                        part_of(dst, here, r)[...] = value
        src, dst = dst, src


def spectrum_reader(chip, above, below):
    def spec_of(z, r):
        if z < FIRST:
            return below[z, r]
        return chip[z - FIRST, r] if z < FIRST + CHIP else above[z - FIRST - CHIP, r]

    return spec_of


def first_kernel(chip, above, below, cof, out, field_a, field_b):
    spec_of = spectrum_reader(chip, above, below)
    for field in (field_a, field_b):
        field[0:8] = jnp.zeros((8, NY), jnp.float32)
        field[8 + WIDE * REALS * REACH :] = jnp.zeros((8, NY), jnp.float32)
    for z in range(REACH):
        for j in range(4):
            for r, value in zip((j, 4 + j), divide(cof, z, j, spec_of(z, j), spec_of(z, 4 + j))):
                part_of(field_a, z, r)[...] = value

    def finish(z, r, value):
        out[z - FIRST, r] = value[4 : 4 + NARROW]

    sweeps(cof, spec_of, field_a, field_b, [(1, 9), (2, 8), (3, 7)], 0, finish)


def second_kernel(chip, above, below, cof, own, high, low, mine, theirs, field_a, field_b):
    core = lax.axis_index("space") % 2
    spec_of = spectrum_reader(chip, above, below)
    for field in (field_a, field_b):
        field[0:8] = jnp.zeros((8, NY), jnp.float32)
        field[8 + WIDE * REALS * 3 * CHIP :] = jnp.zeros((8, NY), jnp.float32)
    edge = jnp.zeros((8, NY), jnp.float32)
    for third, source in enumerate((low, own, high)):
        for plane in range(CHIP):
            for r in range(REALS):
                spot = part_of(field_a, CHIP * third + plane, r)
                spot[0:8] = edge
                spot[WIDE - 8 : WIDE] = edge
                spot[4 : 4 + NARROW] = source[plane, r]
    held = {}

    def finish(z, r, value):
        plane = z - FIRST
        value = value[8 : 8 + OWN]
        if plane < SLAB:
            held[plane, r] = value
        else:
            low_value = held.pop((plane - SLAB, r))
            mine[plane - SLAB, r] = jnp.where(core == 0, low_value, value)
            theirs[plane - SLAB, r] = jnp.where(core == 0, value, low_value)

    sweeps(cof, spec_of, field_a, field_b, [(0, 10), (1, 9), (2, 8), (3, 7)], 1, finish)


def call(kernel, shapes, args, scratch=(), anywhere=False, mib=32):
    vmem = pl.BlockSpec(memory_space=pltpu.VMEM)
    several = isinstance(shapes, list)
    out_shape = [jax.ShapeDtypeStruct(shape, jnp.float32) for shape in (shapes if several else [shapes])]
    return pl.pallas_call(
        kernel,
        out_shape=out_shape if several else out_shape[0],
        in_specs=[pl.BlockSpec(memory_space=pl.ANY) if anywhere else vmem] * len(args),
        out_specs=[vmem] * len(shapes) if several else vmem,
        scratch_shapes=[pltpu.VMEM(dims, jnp.float32) if isinstance(dims, tuple) else dims for dims in scratch],
        compiler_params=pltpu.CompilerParams(vmem_limit_bytes=mib * 1024 * 1024),
    )(*args)


def shards(forcing, iterate, kappa, velocity):
    block = (SLAB, NY, NX)
    previous = lax.ppermute(iterate, "tm", [(i, (i + 1) % WINDOW) for i in range(WINDOW)])
    cores = [(i, i ^ 1) for i in range(2 * CHIPS)]
    upward = [(i, (i + 2) % (2 * CHIPS)) for i in range(2 * CHIPS)]
    downward = [(j, i) for i, j in upward]
    outer, inner = call(
        entry_kernel, [block, block], (iterate, kappa), [pltpu.SemaphoreType.DMA((4,))], anywhere=True, mib=56
    )
    facing = [(i, (i + 1) % (2 * CHIPS)) for i in range(1, 2 * CHIPS, 2)]
    outer = lax.ppermute(outer, "space", facing + [(j, i) for i, j in facing])
    inner = lax.ppermute(inner, "space", cores)
    fields = call(
        fields_kernel,
        (4, SLAB, WIDE, NY),
        (kappa, velocity),
        [(4, SLAB, NY, NX), (8, NX + 16, NY), pltpu.SemaphoreType.DMA((4,))],
        anywhere=True,
    )
    fields_below = lax.ppermute(fields, "space", upward)
    fields_above = lax.ppermute(fields, "space", downward)
    base, rim, value = call(inside_kernel, [block] * 3, (forcing, iterate, kappa, velocity))
    sent = call(
        resid_kernel,
        (WINDOW, SLAB, WIDE, NY),
        (base, rim, value, previous, outer, inner),
        [(SLAB, NX + 16, NY)],
    )
    times = lax.all_to_all(sent, "tm", 0, 0)
    keep, sent = call(
        ahead_kernel,
        [(SLAB, REALS, WIDE, NY), (SLAB * REALS + 24, WIDE, NY)],
        (times, fields, fields_above, fields_below),
    )
    got = lax.ppermute(sent, "space", cores)
    part = (FIRST, REALS, WIDE, NY)
    chip, up, down = call(gather_kernel, [(CHIP, REALS, WIDE, NY), part, part], (keep, got))
    below = lax.ppermute(up, "space", upward)
    above = lax.ppermute(down, "space", downward)
    cof = call(
        prepare_kernel,
        (REACH, 15, WIDE, NY),
        (fields, fields_above, fields_below, got),
        [(4, 3 * CHIP, WIDE, NY)],
    )
    own = call(
        first_kernel,
        (CHIP, REALS, NARROW, NY),
        (chip, above, below, cof),
        [(16 + WIDE * REALS * REACH, NY)] * 2,
    )
    low = lax.ppermute(own, "space", upward)
    high = lax.ppermute(own, "space", downward)
    mine, theirs = call(
        second_kernel,
        [(SLAB, REALS, OWN, NY)] * 2,
        (chip, above, below, cof, own, high, low),
        [(16 + WIDE * REALS * 3 * CHIP, NY)] * 2,
    )
    theirs = lax.ppermute(theirs, "space", cores)
    correction = call(back_kernel, (WINDOW, SLAB, OWN, NY), (mine, theirs))
    correction = lax.all_to_all(correction, "tm", 0, 0)
    return call(update_kernel, (1, SLAB, NY, NX), (correction, iterate))


def solution(mesh):
    in_specs = (
        P("tm", "space", None, None),
        P("tm", "space", None, None),
        P("space", None, None),
        P(None, "space", None, None),
    )
    out_specs = P("tm", "space", None, None)
    return jax.shard_map(shards, mesh=mesh, in_specs=in_specs, out_specs=out_specs, check_vma=False)
```

```python
import functools
import math

import jax
import jax.numpy as jnp
from jax import lax
from jax.experimental import pallas as pl
from jax.experimental.pallas import tpu as pltpu
from jax.sharding import PartitionSpec as P

SWEEPS = 8
ALPHA = 0.05
TIME_STEP = 0.5
WINDOW = 16
DECAY = ALPHA ** (1.0 / WINDOW)
NZ, NY, NX = 32, 128, 256
OWN = NX // WINDOW
WIDE = OWN + 16
SLAB = 2
CHIP = 4
CHIPS = NZ // CHIP
FIRST = 3
EXTRA = 16
REACH = 10
NARROW = OWN + 8
GROUPS = 2
EACH = 2
REALS = 4


def time_scale(n):
    return DECAY**n


def shift_rows():
    rows = []
    for p in range(8):
        angle = 2.0 * math.pi * p / WINDOW
        real = (1.0 - DECAY * math.cos(angle)) / TIME_STEP
        imag = DECAY * math.sin(angle) / TIME_STEP
        other = real if p else (1.0 + DECAY) / TIME_STEP
        rows.append((real, other, imag if p else 0.0))
    return rows


def spectrum_of(times):
    even = [times[j] + times[j + 8] for j in range(8)]
    odd = [times[j] - times[j + 8] for j in range(8)]
    f = [even[j] + even[j + 4] for j in range(4)]
    g = [even[j] - even[j + 4] for j in range(4)]
    parts = [None] * 16
    parts[0] = (f[0] + f[2]) + (f[1] + f[3])
    parts[8] = (f[0] + f[2]) - (f[1] + f[3])
    parts[4] = f[0] - f[2]
    parts[12] = f[3] - f[1]
    root = math.sqrt(0.5)
    less, more = (g[1] - g[3]) * root, (g[1] + g[3]) * root
    parts[2] = g[0] + less
    parts[6] = g[0] - less
    parts[10] = -(g[2] + more)
    parts[14] = g[2] - more
    less = [odd[j] - odd[8 - j] for j in range(1, 4)]
    more = [odd[j] + odd[8 - j] for j in range(1, 4)]
    for k in (1, 3, 5, 7):
        angle = math.pi * k / 8
        parts[k] = odd[0] + sum(math.cos(angle * (j + 1)) * less[j] for j in range(3))
        tail = sum(math.sin(angle * (j + 1)) * more[j] for j in range(3))
        parts[8 + k] = -(tail + odd[4]) if k % 4 == 1 else odd[4] - tail
    return parts


def times_of(parts):
    plus, minus = parts[0] + parts[8], parts[0] - parts[8]
    two = [None if j in (0, 8) else 2.0 * parts[j] for j in range(16)]
    f = [plus + two[4], minus - two[12], plus - two[4], minus + two[12]]
    root = math.sqrt(0.5)
    g = [
        two[2] + two[6],
        root * ((two[2] - two[10]) - (two[6] + two[14])),
        two[14] - two[10],
        root * ((two[6] - two[14]) - (two[2] + two[10])),
    ]
    even = [f[j] + g[j] for j in range(4)] + [f[j] - g[j] for j in range(4)]
    odd = [None] * 8
    odd[0] = (two[1] + two[3]) + (two[5] + two[7])
    odd[4] = (two[11] + two[15]) - (two[9] + two[13])
    for n in range(1, 4):
        c = sum(math.cos(math.pi * p * n / 8) * two[p] for p in (1, 3, 5, 7))
        s = sum(math.sin(math.pi * p * n / 8) * two[8 + p] for p in (1, 3, 5, 7))
        odd[n] = c - s
        odd[8 - n] = -(c + s)
    return [even[n] + odd[n] for n in range(8)] + [even[n] - odd[n] for n in range(8)]


def run_copies(pairs, sems):
    copies = [pltpu.make_async_copy(source, target, sems.at[i]) for i, (source, target) in enumerate(pairs)]
    for copy in copies:
        copy.start()
    return copies


def entry_kernel(iterate, kappa, velocity, first, second, outer, inner, out, held, turned, sems):
    step = lax.axis_index("tm")
    parity = lax.axis_index("space") % 2
    pairs = [(kappa, held.at[0])]
    pairs += [(velocity.at[d], held.at[1 + d]) for d in range(3)]
    pairs += [
        (iterate.at[0, 0], first),
        (iterate.at[0, 1], second),
        (iterate.at[0, parity], outer.at[0]),
        (kappa.at[parity], outer.at[1]),
        (iterate.at[0, 1 - parity], inner.at[0]),
        (kappa.at[1 - parity], inner.at[1]),
    ]
    copies = run_copies(pairs, sems)
    edge = jnp.zeros((8, NY), jnp.float32)
    for field in range(4):
        copies[field].wait()
        for plane in range(SLAB):
            spot = turned.at[SLAB * field + plane]
            spot[0:8] = edge
            spot[8 : 8 + NX] = held[field, plane].T
            spot[8 + NX : 16 + NX] = edge
            out[field, plane] = spot[pl.ds(pl.multiple_of(step * OWN, OWN), WIDE), :]
    for copy in copies[4:]:
        copy.wait()


def inside_kernel(forcing, iterate, kappa, velocity, base, rim):
    row = lax.broadcasted_iota(jnp.int32, (NY, NX), 0)
    lane = lax.broadcasted_iota(jnp.int32, (NY, NX), 1)

    def shifted(array, dim, up):
        extent = NY if dim == 0 else NX
        index = row if dim == 0 else lane
        inside = index < extent - 1 if up else index > 0
        return jnp.where(inside, pltpu.roll(array, extent - 1 if up else 1, dim), 0.0)

    for plane in range(SLAB):
        centre, here = kappa[plane], iterate[0, plane]
        towards = -1.0 if plane == 0 else 1.0
        half = 0.5 * velocity[0, plane]
        face = 0.5 * (centre + kappa[1 - plane])
        diagonal = face + 0.5 * centre
        total = (face + towards * half) * iterate[0, 1 - plane]
        rim[plane] = 0.5 * centre - towards * half
        for dim in range(2):
            half = 0.5 * velocity[1 + dim, plane]
            for up, sign in ((True, -1.0), (False, 1.0)):
                face = 0.5 * (centre + shifted(centre, dim, up))
                diagonal += face
                total += (face + sign * half) * shifted(here, dim, up)
        base[plane] = forcing[0, plane] - here * (1.0 / TIME_STEP) - (diagonal * here - total)


def resid_kernel(base, rim, iterate, first, second, outer, inner, out, turned):
    step = lax.axis_index("tm")
    place = lax.axis_index("space")
    even = place % 2 == 0
    leads = step % 4 == 0
    growth = jnp.exp(jnp.full((1, 1), step.astype(jnp.float32) / WINDOW * math.log(ALPHA), jnp.float32))
    edge = jnp.zeros((8, NY), jnp.float32)

    def turn(spot, array):
        spot[0:8] = edge
        spot[8 : 8 + NX] = array.T
        spot[8 + NX : 16 + NX] = edge

    before = (first, second)
    for plane in range(SLAB):
        side, other = (outer, inner) if plane == 0 else (inner, outer)
        ends = place == 0 if plane == 0 else place == 2 * CHIPS - 1
        here = iterate[0, plane]
        near = jnp.where(ends, 0.0, jnp.where(even, side[0], other[0]))
        far = jnp.where(ends, 0.0, 0.5 * jnp.where(even, side[1], other[1]))
        carried = jnp.where(step == 0 if plane == 0 else leads, 0.0, 1.0 / TIME_STEP)
        resid = base[plane] + before[plane][...] * carried + (rim[plane] + far) * near - far * here
        turn(turned.at[plane], resid * growth)
        for c in range(WINDOW):
            out[c, WIDE * plane : WIDE * (plane + 1)] = turned[plane, OWN * c : OWN * c + WIDE]
    turn(turned.at[SLAB], jnp.where(leads, second[...], iterate[0, 1]))
    skip = jnp.where(leads, 0, 8)
    for c in range(WINDOW):
        for number in range(2):
            start = pl.multiple_of(OWN * c + OWN * number + skip, 8)
            spot = SLAB * WIDE + 8 * number
            out[c, spot : spot + 8] = turned[SLAB, pl.ds(start, 8)]


def ahead_kernel(times, fields, above, below, *outs):
    keeps, sends = outs[:GROUPS], outs[GROUPS:]
    core = lax.axis_index("space") % 2
    for plane in range(SLAB):
        for tile in range(WIDE // 8):
            rows = slice(8 * tile, 8 * tile + 8)
            values = [times[n, WIDE * plane + 8 * tile : WIDE * plane + 8 * tile + 8] for n in range(WINDOW)]
            if plane == 1:
                for n in (4, 8, 12):
                    spot = SLAB * WIDE + 8 * (tile // 2)
                    source = n - 1 if tile % 2 else n - 4
                    values[n] += times[source, spot : spot + 8] * (time_scale(n) / TIME_STEP)
            parts = spectrum_of(values)
            for group, (keep, send) in enumerate(zip(keeps, sends)):
                for r in range(REALS):
                    index = 8 * (r // EACH) + EACH * group + r % EACH
                    low, high = parts[index], parts[index + 4]
                    keep[plane, r, rows] = jnp.where(core == 0, low, high)
                    send[REALS * plane + r, rows] = jnp.where(core == 0, high, low)
    spot = SLAB * REALS
    for source in (below, fields, above):
        for field in range(4):
            for plane in range(SLAB):
                sends[-1][spot] = source[field, plane]
                spot += 1


def gather_kernel(keep, got, chip, up, down):
    core = lax.axis_index("space") % 2
    for r in range(REALS):
        for plane in range(CHIP):
            mine, theirs = keep[plane % SLAB, r], got[REALS * (plane % SLAB) + r]
            value = jnp.where(core == plane // SLAB, mine, theirs)
            chip[plane, r] = value
            if plane >= CHIP - FIRST:
                up[plane - (CHIP - FIRST), r] = value
            if plane < FIRST:
                down[plane, r] = value


def back_kernel(*refs):
    mines, theirs, out = refs[:GROUPS], refs[GROUPS:-1], refs[-1]
    core = lax.axis_index("space") % 2
    for plane in range(SLAB):
        for tile in range(OWN // 8):
            rows = slice(8 * tile, 8 * tile + 8)
            parts = [None] * 16
            for group in range(GROUPS):
                for r in range(REALS):
                    index = 8 * (r // EACH) + EACH * group + r % EACH
                    one, two = mines[group][plane, r, rows], theirs[group][plane, r, rows]
                    parts[index] = jnp.where(core == 0, one, two)
                    parts[index + 4] = jnp.where(core == 0, two, one)
            values = times_of(parts)
            for n in range(WINDOW):
                out[n, plane, rows] = values[n] * (time_scale(-n) / WINDOW)


def update_kernel(correction, iterate, out):
    for plane in range(SLAB):
        turned = correction[:, plane].reshape(NX, NY).T
        out[0, plane] = iterate[0, plane] + turned


def prepare_kernel(fields, above, below, got, cof, held):
    place = lax.axis_index("space")
    core, chip = place % 2, place // 2
    start = lax.axis_index("tm") * OWN - 8
    column = start + lax.broadcasted_iota(jnp.int32, (WIDE, NY), 0)
    lane = lax.broadcasted_iota(jnp.int32, (WIDE, NY), 1)
    rows = shift_rows()
    shifts = [[jnp.where(core == 0, rows[j][i], rows[4 + j][i]) for i in range(3)] for j in range(4)]
    spot = SLAB * REALS
    for third, source in enumerate((below, fields, above)):
        for field in range(4):
            for plane in range(SLAB):
                value, other = source[field, plane], got[spot]
                spot += 1
                if field == 0 and third != 1:
                    outside = chip == (0 if third == 0 else CHIPS - 1)
                    value, other = jnp.where(outside, 0.0, value), jnp.where(outside, 0.0, other)
                held[field, CHIP * third + plane] = jnp.where(core == 0, value, other)
                held[field, CHIP * third + SLAB + plane] = jnp.where(core == 0, other, value)
    for z in range(REACH):
        spot = z + 1
        centre = held[0, spot]
        half = [0.5 * held[1 + d, spot] for d in range(3)]
        up_z = 0.5 * (centre + held[0, spot + 1])
        down_z = 0.5 * (centre + held[0, spot - 1])
        up_y = 0.5 * (centre + jnp.where(lane < NY - 1, pltpu.roll(centre, NY - 1, 1), 0.0))
        down_y = 0.5 * (centre + jnp.where(lane > 0, pltpu.roll(centre, 1, 1), 0.0))
        up_x = 0.5 * (centre + pltpu.roll(centre, WIDE - 1, 0))
        down_x = 0.5 * (centre + pltpu.roll(centre, 1, 0))
        diagonal = up_z + down_z + up_y + down_y + up_x + down_x
        plus_z, minus_z = up_z - half[0], down_z + half[0]
        if spot == 2 * CHIP - 1:
            plus_z = jnp.where(chip == CHIPS - 1, 0.0, plus_z)
        if spot == CHIP:
            minus_z = jnp.where(chip == 0, 0.0, minus_z)
        cof[z, 0] = plus_z
        cof[z, 1] = minus_z
        cof[z, 2] = jnp.where(lane < NY - 1, up_y - half[1], 0.0)
        cof[z, 3] = jnp.where(lane > 0, down_y + half[1], 0.0)
        cof[z, 4] = jnp.where(column < NX - 1, up_x - half[2], 0.0)
        cof[z, 5] = jnp.where(column > 0, down_x + half[2], 0.0)
        for j, (real, other, imag) in enumerate(shifts):
            den = real + diagonal
            scale = 1.0 / (den * den + imag * imag)
            cof[z, 6 + 2 * j] = den * scale
            cof[z, 7 + 2 * j] = -imag * scale
            if j == 0:
                den = other + diagonal
                cof[z, 14] = den / (den * den + imag * imag)


def divide(cof, z, j, total_real, total_imag):
    inv_real, inv_imag = cof[z, 6 + 2 * j], cof[z, 7 + 2 * j]
    inv_other = cof[z, 14] if j == 0 else inv_real
    return (
        total_real * inv_real - total_imag * inv_imag,
        total_real * inv_imag + total_imag * inv_other,
    )


def part_of(field, z, r, ahead=0):
    start = 8 + WIDE * (REALS * z + r) + ahead
    return field.at[start : start + WIDE]


def sweeps(group, cof, spec_of, src, dst, planes, shift, finish):
    for number, (first, end) in enumerate(planes):
        for z in range(first, end):
            here = z + shift
            for j in range(EACH):
                totals = []
                for r in (j, EACH + j):
                    centre = part_of(src, here, r)[...]
                    total = cof[z, 0] * part_of(src, here + 1, r)[...] + cof[z, 1] * part_of(src, here - 1, r)[...]
                    total += cof[z, 2] * pltpu.roll(centre, NY - 1, 1) + cof[z, 3] * pltpu.roll(centre, 1, 1)
                    total += cof[z, 4] * part_of(src, here, r, 1)[...] + cof[z, 5] * part_of(src, here, r, -1)[...]
                    totals.append(total + spec_of(z, r))
                for r, value in zip((j, EACH + j), divide(cof, z, EACH * group + j, *totals)):
                    if number == len(planes) - 1:
                        finish(z, r, value)
                    else:
                        part_of(dst, here, r)[...] = value
        src, dst = dst, src


def spectrum_reader(chip, above, below):
    def spec_of(z, r):
        if z < FIRST:
            return below[z, r]
        return chip[z - FIRST, r] if z < FIRST + CHIP else above[z - FIRST - CHIP, r]

    return spec_of


def first_kernel(group, chip, above, below, cof, out, field_a, field_b):
    spec_of = spectrum_reader(chip, above, below)
    for field in (field_a, field_b):
        field[0:8] = jnp.zeros((8, NY), jnp.float32)
        field[8 + WIDE * REALS * REACH :] = jnp.zeros((8, NY), jnp.float32)
    for z in range(REACH):
        for j in range(EACH):
            values = divide(cof, z, EACH * group + j, spec_of(z, j), spec_of(z, EACH + j))
            for r, value in zip((j, EACH + j), values):
                part_of(field_a, z, r)[...] = value

    def finish(z, r, value):
        out[z - FIRST, r] = value[4 : 4 + NARROW]

    sweeps(group, cof, spec_of, field_a, field_b, [(1, 9), (2, 8), (3, 7)], 0, finish)


def second_kernel(group, chip, above, below, cof, own, high, low, mine, theirs, field_a, field_b):
    core = lax.axis_index("space") % 2
    spec_of = spectrum_reader(chip, above, below)
    for field in (field_a, field_b):
        field[0:8] = jnp.zeros((8, NY), jnp.float32)
        field[8 + WIDE * REALS * 3 * CHIP :] = jnp.zeros((8, NY), jnp.float32)
    edge = jnp.zeros((8, NY), jnp.float32)
    for third, source in enumerate((low, own, high)):
        for plane in range(CHIP):
            for r in range(REALS):
                spot = part_of(field_a, CHIP * third + plane, r)
                spot[0:8] = edge
                spot[WIDE - 8 : WIDE] = edge
                spot[4 : 4 + NARROW] = source[plane, r]
    held = {}

    def finish(z, r, value):
        plane = z - FIRST
        value = value[8 : 8 + OWN]
        if plane < SLAB:
            held[plane, r] = value
        else:
            low_value = held.pop((plane - SLAB, r))
            mine[plane - SLAB, r] = jnp.where(core == 0, low_value, value)
            theirs[plane - SLAB, r] = jnp.where(core == 0, value, low_value)

    sweeps(group, cof, spec_of, field_a, field_b, [(0, 10), (1, 9), (2, 8), (3, 7)], 1, finish)


def call(kernel, shapes, args, scratch=(), anywhere=False, mib=32):
    vmem = pl.BlockSpec(memory_space=pltpu.VMEM)
    several = isinstance(shapes, list)
    out_shape = [jax.ShapeDtypeStruct(shape, jnp.float32) for shape in (shapes if several else [shapes])]
    return pl.pallas_call(
        kernel,
        out_shape=out_shape if several else out_shape[0],
        in_specs=[pl.BlockSpec(memory_space=pl.ANY) if anywhere else vmem] * len(args),
        out_specs=[vmem] * len(shapes) if several else vmem,
        scratch_shapes=[pltpu.VMEM(dims, jnp.float32) if isinstance(dims, tuple) else dims for dims in scratch],
        compiler_params=pltpu.CompilerParams(vmem_limit_bytes=mib * 1024 * 1024),
    )(*args)


def shards(forcing, iterate, kappa, velocity):
    single, block = (NY, NX), (SLAB, NY, NX)
    cores = [(i, i ^ 1) for i in range(2 * CHIPS)]
    upward = [(i, (i + 2) % (2 * CHIPS)) for i in range(2 * CHIPS)]
    downward = [(j, i) for i, j in upward]
    facing = [(i, (i + 1) % (2 * CHIPS)) for i in range(1, 2 * CHIPS, 2)]
    facing += [(j, i) for i, j in facing]
    first, second, outer, inner, fields = call(
        entry_kernel,
        [single, single, block, block, (4, SLAB, WIDE, NY)],
        (iterate, kappa, velocity),
        [(4, *block), (8, NX + 16, NY), pltpu.SemaphoreType.DMA((10,))],
        anywhere=True,
        mib=56,
    )
    first = lax.ppermute(first, "tm", [(i, (i + 1) % WINDOW) for i in range(WINDOW)])
    second = lax.ppermute(second, "tm", [(i, i // 4 * 4 + (i + 1) % 4) for i in range(WINDOW)])
    outer = lax.ppermute(outer, "space", facing)
    inner = lax.ppermute(inner, "space", cores)
    fields_below = lax.ppermute(fields, "space", upward)
    fields_above = lax.ppermute(fields, "space", downward)
    base, rim = call(inside_kernel, [block, block], (forcing, iterate, kappa, velocity))
    first, fields_below, fields_above = lax.optimization_barrier((first, fields_below, fields_above))
    sent = call(
        resid_kernel,
        (WINDOW, SLAB * WIDE + EXTRA, NY),
        (base, rim, iterate, first, second, outer, inner),
        [(SLAB + 1, NX + 16, NY)],
    )
    times = lax.all_to_all(sent, "tm", 0, 0)
    parts = call(
        ahead_kernel,
        [(SLAB, REALS, WIDE, NY)] * GROUPS
        + [(SLAB * REALS + (24 if group == GROUPS - 1 else 0), WIDE, NY) for group in range(GROUPS)],
        (times, fields, fields_above, fields_below),
    )
    got = [lax.ppermute(sent, "space", cores) for sent in parts[GROUPS:]]
    chips, aboves, belows = [], [], []
    for group in range(GROUPS):
        shape = (FIRST, REALS, WIDE, NY)
        chip, up, down = call(gather_kernel, [(CHIP, REALS, WIDE, NY), shape, shape], (parts[group], got[group]))
        chips.append(chip)
        belows.append(lax.ppermute(up, "space", upward))
        aboves.append(lax.ppermute(down, "space", downward))
    cof = call(
        prepare_kernel,
        (REACH, 15, WIDE, NY),
        (fields, fields_above, fields_below, got[-1]),
        [(4, 3 * CHIP, WIDE, NY)],
    )
    owns, lows, highs = [], [], []
    for group in range(GROUPS):
        own = call(
            functools.partial(first_kernel, group),
            (CHIP, REALS, NARROW, NY),
            (chips[group], aboves[group], belows[group], cof),
            [(16 + WIDE * REALS * REACH, NY)] * 2,
        )
        owns.append(own)
        lows.append(lax.ppermute(own, "space", upward))
        highs.append(lax.ppermute(own, "space", downward))
    mines, theirs = [], []
    for group in range(GROUPS):
        mine, other = call(
            functools.partial(second_kernel, group),
            [(SLAB, REALS, OWN, NY)] * 2,
            (chips[group], aboves[group], belows[group], cof, owns[group], highs[group], lows[group]),
            [(16 + WIDE * REALS * 3 * CHIP, NY)] * 2,
        )
        mines.append(mine)
        theirs.append(lax.ppermute(other, "space", cores))
    correction = call(back_kernel, (WINDOW, SLAB, OWN, NY), (*mines, *theirs))
    correction = lax.all_to_all(correction, "tm", 0, 0)
    return call(update_kernel, (1, SLAB, NY, NX), (correction, iterate))


def solution(mesh):
    in_specs = (
        P("tm", "space", None, None),
        P("tm", "space", None, None),
        P("space", None, None),
        P(None, "space", None, None),
    )
    out_specs = P("tm", "space", None, None)
    return jax.shard_map(shards, mesh=mesh, in_specs=in_specs, out_specs=out_specs, check_vma=False)
```

```python
import functools
import math

import jax
import jax.numpy as jnp
from jax import lax
from jax.experimental import pallas as pl
from jax.experimental.pallas import tpu as pltpu
from jax.sharding import PartitionSpec as P

SWEEPS = 8
ALPHA = 0.05
TIME_STEP = 0.5
WINDOW = 16
DECAY = ALPHA ** (1.0 / WINDOW)
NZ, NY, NX = 32, 128, 256
OWN = NX // WINDOW
WIDE = OWN + 16
SLAB = 2
CHIP = 4
CHIPS = NZ // CHIP
FIRST = 3
EXTRA = 16
REACH = 10
NARROW = OWN + 8
GROUPS = 2
EACH = 2
REALS = 4


def time_scale(n):
    return DECAY**n


def shift_rows():
    rows = []
    for p in range(8):
        angle = 2.0 * math.pi * p / WINDOW
        real = (1.0 - DECAY * math.cos(angle)) / TIME_STEP
        imag = DECAY * math.sin(angle) / TIME_STEP
        other = real if p else (1.0 + DECAY) / TIME_STEP
        rows.append((real, other, imag if p else 0.0))
    return rows


def spectrum_of(times):
    even = [times[j] + times[j + 8] for j in range(8)]
    odd = [times[j] - times[j + 8] for j in range(8)]
    f = [even[j] + even[j + 4] for j in range(4)]
    g = [even[j] - even[j + 4] for j in range(4)]
    parts = [None] * 16
    parts[0] = (f[0] + f[2]) + (f[1] + f[3])
    parts[8] = (f[0] + f[2]) - (f[1] + f[3])
    parts[4] = f[0] - f[2]
    parts[12] = f[3] - f[1]
    root = math.sqrt(0.5)
    less, more = (g[1] - g[3]) * root, (g[1] + g[3]) * root
    parts[2] = g[0] + less
    parts[6] = g[0] - less
    parts[10] = -(g[2] + more)
    parts[14] = g[2] - more
    less = [odd[j] - odd[8 - j] for j in range(1, 4)]
    more = [odd[j] + odd[8 - j] for j in range(1, 4)]
    for k in (1, 3, 5, 7):
        angle = math.pi * k / 8
        parts[k] = odd[0] + sum(math.cos(angle * (j + 1)) * less[j] for j in range(3))
        tail = sum(math.sin(angle * (j + 1)) * more[j] for j in range(3))
        parts[8 + k] = -(tail + odd[4]) if k % 4 == 1 else odd[4] - tail
    return parts


def times_of(parts):
    plus, minus = parts[0] + parts[8], parts[0] - parts[8]
    two = [None if j in (0, 8) else 2.0 * parts[j] for j in range(16)]
    f = [plus + two[4], minus - two[12], plus - two[4], minus + two[12]]
    root = math.sqrt(0.5)
    g = [
        two[2] + two[6],
        root * ((two[2] - two[10]) - (two[6] + two[14])),
        two[14] - two[10],
        root * ((two[6] - two[14]) - (two[2] + two[10])),
    ]
    even = [f[j] + g[j] for j in range(4)] + [f[j] - g[j] for j in range(4)]
    odd = [None] * 8
    odd[0] = (two[1] + two[3]) + (two[5] + two[7])
    odd[4] = (two[11] + two[15]) - (two[9] + two[13])
    for n in range(1, 4):
        c = sum(math.cos(math.pi * p * n / 8) * two[p] for p in (1, 3, 5, 7))
        s = sum(math.sin(math.pi * p * n / 8) * two[8 + p] for p in (1, 3, 5, 7))
        odd[n] = c - s
        odd[8 - n] = -(c + s)
    return [even[n] + odd[n] for n in range(8)] + [even[n] - odd[n] for n in range(8)]


def run_copies(pairs, sems):
    copies = [pltpu.make_async_copy(source, target, sems.at[i]) for i, (source, target) in enumerate(pairs)]
    for copy in copies:
        copy.start()
    return copies


def entry_kernel(iterate, kappa, velocity, outer, inner, out, held, turned, sems):
    step = lax.axis_index("tm")
    parity = lax.axis_index("space") % 2
    pairs = [(kappa, held.at[0])]
    pairs += [(velocity.at[d], held.at[1 + d]) for d in range(3)]
    pairs += [
        (iterate.at[0, parity], outer.at[0]),
        (kappa.at[parity], outer.at[1]),
        (iterate.at[0, 1 - parity], inner.at[0]),
        (kappa.at[1 - parity], inner.at[1]),
    ]
    copies = run_copies(pairs, sems)
    edge = jnp.zeros((8, NY), jnp.float32)
    for field in range(4):
        copies[field].wait()
        for plane in range(SLAB):
            spot = turned.at[SLAB * field + plane]
            spot[0:8] = edge
            spot[8 : 8 + NX] = held[field, plane].T
            spot[8 + NX : 16 + NX] = edge
            out[field, plane] = spot[pl.ds(pl.multiple_of(step * OWN, OWN), WIDE), :]
    for copy in copies[4:]:
        copy.wait()


def inside_kernel(forcing_hbm, iterate_hbm, kappa_hbm, velocity_hbm, base, rim, *scratch):
    forcing, iterate, kappa, velocity, sems = scratch
    pairs = [(kappa_hbm, kappa), (iterate_hbm, iterate), (velocity_hbm, velocity), (forcing_hbm, forcing)]
    for copy in run_copies(pairs, sems):
        copy.wait()
    row = lax.broadcasted_iota(jnp.int32, (NY, NX), 0)
    lane = lax.broadcasted_iota(jnp.int32, (NY, NX), 1)

    def shifted(array, dim, up):
        extent = NY if dim == 0 else NX
        index = row if dim == 0 else lane
        inside = index < extent - 1 if up else index > 0
        return jnp.where(inside, pltpu.roll(array, extent - 1 if up else 1, dim), 0.0)

    for plane in range(SLAB):
        centre, here = kappa[plane], iterate[0, plane]
        towards = -1.0 if plane == 0 else 1.0
        half = 0.5 * velocity[0, plane]
        face = 0.5 * (centre + kappa[1 - plane])
        diagonal = face + 0.5 * centre
        total = (face + towards * half) * iterate[0, 1 - plane]
        rim[plane] = 0.5 * centre - towards * half
        for dim in range(2):
            half = 0.5 * velocity[1 + dim, plane]
            for up, sign in ((True, -1.0), (False, 1.0)):
                face = 0.5 * (centre + shifted(centre, dim, up))
                diagonal += face
                total += (face + sign * half) * shifted(here, dim, up)
        base[plane] = forcing[0, plane] - here * (1.0 / TIME_STEP) - (diagonal * here - total)


def resid_kernel(base, rim, iterate, previous, outer, inner, out, turned):
    step = lax.axis_index("tm")
    place = lax.axis_index("space")
    even = place % 2 == 0
    leads = step % 4 == 0
    growth = jnp.exp(jnp.full((1, 1), step.astype(jnp.float32) / WINDOW * math.log(ALPHA), jnp.float32))
    edge = jnp.zeros((8, NY), jnp.float32)

    def turn(spot, array):
        spot[0:8] = edge
        spot[8 : 8 + NX] = array.T
        spot[8 + NX : 16 + NX] = edge

    carried = jnp.where(leads, 0.0, 1.0 / TIME_STEP)
    skip = jnp.where(leads, 0, 8)
    for plane in range(SLAB):
        side, other = (outer, inner) if plane == 0 else (inner, outer)
        ends = place == 0 if plane == 0 else place == 2 * CHIPS - 1
        here = iterate[0, plane]
        near = jnp.where(ends, 0.0, jnp.where(even, side[0], other[0]))
        far = jnp.where(ends, 0.0, 0.5 * jnp.where(even, side[1], other[1]))
        resid = base[plane] + previous[0, plane] * carried + (rim[plane] + far) * near - far * here
        turn(turned.at[plane], resid * growth)
        for c in range(WINDOW):
            out[c, WIDE * plane : WIDE * (plane + 1)] = turned[plane, OWN * c : OWN * c + WIDE]
        turn(turned.at[SLAB + plane], jnp.where(leads, previous[0, plane], here))
        for c in range(WINDOW):
            for number in range(2):
                start = pl.multiple_of(OWN * c + OWN * number + skip, 8)
                spot = SLAB * WIDE + EXTRA * plane + 8 * number
                out[c, spot : spot + 8] = turned[SLAB + plane, pl.ds(start, 8)]


def ahead_kernel(times, *outs):
    keeps, sends = outs[:GROUPS], outs[GROUPS:]
    core = lax.axis_index("space") % 2
    for plane in range(SLAB):
        for tile in range(WIDE // 8):
            rows = slice(8 * tile, 8 * tile + 8)
            values = [times[n, WIDE * plane + 8 * tile : WIDE * plane + 8 * tile + 8] for n in range(WINDOW)]
            spot = SLAB * WIDE + EXTRA * plane + 8 * (tile // 2)
            for n in (4, 8, 12):
                source = n - 1 if tile % 2 else n - 4
                values[n] += times[source, spot : spot + 8] * (time_scale(n) / TIME_STEP)
            parts = spectrum_of(values)
            for group, (keep, send) in enumerate(zip(keeps, sends)):
                for r in range(REALS):
                    index = 8 * (r // EACH) + EACH * group + r % EACH
                    low, high = parts[index], parts[index + 4]
                    keep[plane, r, rows] = jnp.where(core == 0, low, high)
                    send[REALS * plane + r, rows] = jnp.where(core == 0, high, low)


def pick(even, odd):
    return jnp.where(lax.axis_index("space") // 2 % 2 == 0, even, odd)


def gather_kernel(keep, got, chip, pair, other):
    core = lax.axis_index("space") % 2
    for r in range(REALS):
        values = []
        for plane in range(CHIP):
            mine, theirs = keep[plane % SLAB, r], got[REALS * (plane % SLAB) + r]
            values.append(jnp.where(core == plane // SLAB, mine, theirs))
            chip[plane, r] = values[plane]
        for plane in range(FIRST):
            pair[plane, r] = pick(values[plane + 1], values[plane])
            other[plane, r] = pick(values[plane], values[plane + 1])


def pack_kernel(pair, fields, other, out):
    for third, source in enumerate((pair, fields, other)):
        for field in range(4):
            for plane in range(SLAB):
                out[third, field, plane] = source[field, plane]


def back_kernel(*refs):
    mines, theirs, out = refs[:GROUPS], refs[GROUPS:-1], refs[-1]
    core = lax.axis_index("space") % 2
    for plane in range(SLAB):
        for tile in range(OWN // 8):
            rows = slice(8 * tile, 8 * tile + 8)
            parts = [None] * 16
            for group in range(GROUPS):
                for r in range(REALS):
                    index = 8 * (r // EACH) + EACH * group + r % EACH
                    one, two = mines[group][plane, r, rows], theirs[group][plane, r, rows]
                    parts[index] = jnp.where(core == 0, one, two)
                    parts[index + 4] = jnp.where(core == 0, two, one)
            values = times_of(parts)
            for n in range(WINDOW):
                out[n, plane, rows] = values[n] * (time_scale(-n) / WINDOW)


def update_kernel(correction, iterate, out):
    for plane in range(SLAB):
        turned = correction[:, plane].reshape(NX, NY).T
        out[0, plane] = iterate[0, plane] + turned


def prepare_kernel(pair, fields, other, got, cof, held):
    place = lax.axis_index("space")
    core, chip = place % 2, place // 2
    start = lax.axis_index("tm") * OWN - 8
    column = start + lax.broadcasted_iota(jnp.int32, (WIDE, NY), 0)
    lane = lax.broadcasted_iota(jnp.int32, (WIDE, NY), 1)
    rows = shift_rows()
    shifts = [[jnp.where(core == 0, rows[j][i], rows[4 + j][i]) for i in range(3)] for j in range(4)]
    for third in range(3):
        for field in range(4):
            for plane in range(SLAB):
                if third == 1:
                    value, partner = fields[field, plane], got[1, field, plane]
                else:
                    sources = [(pair[field, plane], got[0, field, plane]), (other[field, plane], got[2, field, plane])]
                    below, above = sources[::-1], sources
                    even, odd = below if third == 0 else above
                    value, partner = pick(even[0], odd[0]), pick(even[1], odd[1])
                    if field == 0:
                        outside = chip == (0 if third == 0 else CHIPS - 1)
                        value, partner = jnp.where(outside, 0.0, value), jnp.where(outside, 0.0, partner)
                held[field, CHIP * third + plane] = jnp.where(core == 0, value, partner)
                held[field, CHIP * third + SLAB + plane] = jnp.where(core == 0, partner, value)
    for z in range(REACH):
        spot = z + 1
        centre = held[0, spot]
        half = [0.5 * held[1 + d, spot] for d in range(3)]
        up_z = 0.5 * (centre + held[0, spot + 1])
        down_z = 0.5 * (centre + held[0, spot - 1])
        up_y = 0.5 * (centre + jnp.where(lane < NY - 1, pltpu.roll(centre, NY - 1, 1), 0.0))
        down_y = 0.5 * (centre + jnp.where(lane > 0, pltpu.roll(centre, 1, 1), 0.0))
        up_x = 0.5 * (centre + pltpu.roll(centre, WIDE - 1, 0))
        down_x = 0.5 * (centre + pltpu.roll(centre, 1, 0))
        diagonal = up_z + down_z + up_y + down_y + up_x + down_x
        plus_z, minus_z = up_z - half[0], down_z + half[0]
        if spot == 2 * CHIP - 1:
            plus_z = jnp.where(chip == CHIPS - 1, 0.0, plus_z)
        if spot == CHIP:
            minus_z = jnp.where(chip == 0, 0.0, minus_z)
        cof[z, 0] = plus_z
        cof[z, 1] = minus_z
        cof[z, 2] = jnp.where(lane < NY - 1, up_y - half[1], 0.0)
        cof[z, 3] = jnp.where(lane > 0, down_y + half[1], 0.0)
        cof[z, 4] = jnp.where(column < NX - 1, up_x - half[2], 0.0)
        cof[z, 5] = jnp.where(column > 0, down_x + half[2], 0.0)
        for j, (real, other, imag) in enumerate(shifts):
            den = real + diagonal
            scale = 1.0 / (den * den + imag * imag)
            cof[z, 6 + 2 * j] = den * scale
            cof[z, 7 + 2 * j] = -imag * scale
            if j == 0:
                den = other + diagonal
                cof[z, 14] = den / (den * den + imag * imag)


def divide(cof, z, j, total_real, total_imag):
    inv_real, inv_imag = cof[z, 6 + 2 * j], cof[z, 7 + 2 * j]
    inv_other = cof[z, 14] if j == 0 else inv_real
    return (
        total_real * inv_real - total_imag * inv_imag,
        total_real * inv_imag + total_imag * inv_other,
    )


def part_of(field, z, r, ahead=0):
    start = 8 + WIDE * (REALS * z + r) + ahead
    return field.at[start : start + WIDE]


def sweeps(group, cof, spec_of, src, dst, planes, shift, finish):
    for number, (first, end) in enumerate(planes):
        for z in range(first, end):
            here = z + shift
            for j in range(EACH):
                totals = []
                for r in (j, EACH + j):
                    centre = part_of(src, here, r)[...]
                    total = cof[z, 0] * part_of(src, here + 1, r)[...] + cof[z, 1] * part_of(src, here - 1, r)[...]
                    total += cof[z, 2] * pltpu.roll(centre, NY - 1, 1) + cof[z, 3] * pltpu.roll(centre, 1, 1)
                    total += cof[z, 4] * part_of(src, here, r, 1)[...] + cof[z, 5] * part_of(src, here, r, -1)[...]
                    totals.append(total + spec_of(z, r))
                for r, value in zip((j, EACH + j), divide(cof, z, EACH * group + j, *totals)):
                    if number == len(planes) - 1:
                        finish(z, r, value)
                    else:
                        part_of(dst, here, r)[...] = value
        src, dst = dst, src


def spectrum_reader(chip, pair, other):
    def spec_of(z, r):
        if z < FIRST:
            return pick(other[z, r], pair[z, r])
        if z < FIRST + CHIP:
            return chip[z - FIRST, r]
        return pick(pair[z - FIRST - CHIP, r], other[z - FIRST - CHIP, r])

    return spec_of


def first_kernel(group, chip, pair, other, cof, out, field_a, field_b):
    spec_of = spectrum_reader(chip, pair, other)
    for field in (field_a, field_b):
        field[0:8] = jnp.zeros((8, NY), jnp.float32)
        field[8 + WIDE * REALS * REACH :] = jnp.zeros((8, NY), jnp.float32)
    for z in range(REACH):
        for j in range(EACH):
            values = divide(cof, z, EACH * group + j, spec_of(z, j), spec_of(z, EACH + j))
            for r, value in zip((j, EACH + j), values):
                part_of(field_a, z, r)[...] = value

    def finish(z, r, value):
        out[z - FIRST, r] = value[4 : 4 + NARROW]

    sweeps(group, cof, spec_of, field_a, field_b, [(1, 9), (2, 8), (3, 7)], 0, finish)


def second_kernel(group, chip, pair, other, cof, own, pair_own, other_own, mine, theirs, field_a, field_b):
    core = lax.axis_index("space") % 2
    spec_of = spectrum_reader(chip, pair, other)
    for field in (field_a, field_b):
        field[0:8] = jnp.zeros((8, NY), jnp.float32)
        field[8 + WIDE * REALS * 3 * CHIP :] = jnp.zeros((8, NY), jnp.float32)
    edge = jnp.zeros((8, NY), jnp.float32)
    sources = ((other_own, pair_own), (own, own), (pair_own, other_own))
    for third, (even, odd) in enumerate(sources):
        for plane in range(CHIP):
            for r in range(REALS):
                spot = part_of(field_a, CHIP * third + plane, r)
                spot[0:8] = edge
                spot[WIDE - 8 : WIDE] = edge
                spot[4 : 4 + NARROW] = own[plane, r] if third == 1 else pick(even[plane, r], odd[plane, r])
    held = {}

    def finish(z, r, value):
        plane = z - FIRST
        value = value[8 : 8 + OWN]
        if plane < SLAB:
            held[plane, r] = value
        else:
            low_value = held.pop((plane - SLAB, r))
            mine[plane - SLAB, r] = jnp.where(core == 0, low_value, value)
            theirs[plane - SLAB, r] = jnp.where(core == 0, value, low_value)

    sweeps(group, cof, spec_of, field_a, field_b, [(0, 10), (1, 9), (2, 8), (3, 7)], 1, finish)


INSIDE_MIB = 53.25


def call(kernel, shapes, args, scratch=(), anywhere=False, mib=32):
    vmem = pl.BlockSpec(memory_space=pltpu.VMEM)
    several = isinstance(shapes, list)
    out_shape = [jax.ShapeDtypeStruct(shape, jnp.float32) for shape in (shapes if several else [shapes])]
    return pl.pallas_call(
        kernel,
        out_shape=out_shape if several else out_shape[0],
        in_specs=[pl.BlockSpec(memory_space=pl.ANY) if anywhere else vmem] * len(args),
        out_specs=[vmem] * len(shapes) if several else vmem,
        scratch_shapes=[pltpu.VMEM(dims, jnp.float32) if isinstance(dims, tuple) else dims for dims in scratch],
        compiler_params=pltpu.CompilerParams(vmem_limit_bytes=int(mib * 1024 * 1024)),
    )(*args)


def shards(forcing, iterate, kappa, velocity):
    block = (SLAB, NY, NX)
    cores = [(i, i ^ 1) for i in range(2 * CHIPS)]
    pairs = [(i, i ^ 2) for i in range(2 * CHIPS)]
    others = [(i, (i + 2) % (2 * CHIPS)) for i in range(2 * CHIPS) if i // 2 % 2]
    others += [(j, i) for i, j in others]
    facing = [(i, (i + 1) % (2 * CHIPS)) for i in range(1, 2 * CHIPS, 2)]
    facing += [(j, i) for i, j in facing]
    previous = lax.ppermute(iterate, "tm", [(i, i // 4 * 4 + (i + 1) % 4) for i in range(WINDOW)])
    outer, inner, fields = call(
        entry_kernel,
        [block, block, (4, SLAB, WIDE, NY)],
        (iterate, kappa, velocity),
        [(4, *block), (8, NX + 16, NY), pltpu.SemaphoreType.DMA((8,))],
        anywhere=True,
        mib=53.25,
    )
    outer = lax.ppermute(outer, "space", facing)
    inner = lax.ppermute(inner, "space", cores)
    fields, inner = lax.optimization_barrier((fields, inner))
    fields_pair = lax.ppermute(fields, "space", pairs)
    fields_other = lax.ppermute(fields, "space", others)
    base, rim = call(
        inside_kernel,
        [block, block],
        (forcing, iterate, kappa, velocity),
        [(1, *block), (1, *block), block, (3, *block), pltpu.SemaphoreType.DMA((4,))],
        anywhere=True,
        mib=INSIDE_MIB,
    )
    outer, fields_pair, fields_other = lax.optimization_barrier((outer, fields_pair, fields_other))
    sent = call(
        resid_kernel,
        (WINDOW, SLAB * (WIDE + EXTRA), NY),
        (base, rim, iterate, previous, outer, inner),
        [(2 * SLAB, NX + 16, NY)],
    )
    times = lax.all_to_all(sent, "tm", 0, 0)
    parts = call(
        ahead_kernel,
        [(SLAB, REALS, WIDE, NY)] * GROUPS
        + [(SLAB * REALS, WIDE, NY)] * GROUPS,
        (times,),
    )
    got = [lax.ppermute(sent, "space", cores) for sent in parts[GROUPS:]]
    chips, pair_specs, other_specs = [], [], []
    for group in range(GROUPS):
        shape = (FIRST, REALS, WIDE, NY)
        chip, pair, other = call(gather_kernel, [(CHIP, REALS, WIDE, NY), shape, shape], (parts[group], got[group]))
        chips.append(chip)
        pair_specs.append(lax.ppermute(pair, "space", pairs))
        other_specs.append(lax.ppermute(other, "space", others))
    fields, chips[-1] = lax.optimization_barrier((fields, chips[-1]))
    held = call(pack_kernel, (3, 4, SLAB, WIDE, NY), (fields_pair, fields, fields_other))
    held = lax.ppermute(held, "space", cores)
    cof = call(
        prepare_kernel,
        (REACH, 15, WIDE, NY),
        (fields_pair, fields, fields_other, held),
        [(4, 3 * CHIP, WIDE, NY)],
    )
    owns, pair_owns, other_owns = [], [], []
    for group in range(GROUPS):
        own = call(
            functools.partial(first_kernel, group),
            (CHIP, REALS, NARROW, NY),
            (chips[group], pair_specs[group], other_specs[group], cof),
            [(16 + WIDE * REALS * REACH, NY)] * 2,
        )
        owns.append(own)
        pair_owns.append(lax.ppermute(own, "space", pairs))
        other_owns.append(lax.ppermute(own, "space", others))
    mines, theirs = [], []
    for group in range(GROUPS):
        mine, other = call(
            functools.partial(second_kernel, group),
            [(SLAB, REALS, OWN, NY)] * 2,
            (
                *(chips[group], pair_specs[group], other_specs[group], cof),
                *(owns[group], pair_owns[group], other_owns[group]),
            ),
            [(16 + WIDE * REALS * 3 * CHIP, NY)] * 2,
        )
        mines.append(mine)
        theirs.append(lax.ppermute(other, "space", cores))
    correction = call(back_kernel, (WINDOW, SLAB, OWN, NY), (*mines, *theirs))
    correction = lax.all_to_all(correction, "tm", 0, 0)
    return call(update_kernel, (1, SLAB, NY, NX), (correction, iterate))


def solution(mesh):
    in_specs = (
        P("tm", "space", None, None),
        P("tm", "space", None, None),
        P("space", None, None),
        P(None, "space", None, None),
    )
    out_specs = P("tm", "space", None, None)
    return jax.shard_map(shards, mesh=mesh, in_specs=in_specs, out_specs=out_specs, check_vma=False)
```

```python
import functools
import math

import jax
import jax.numpy as jnp
from jax import lax
from jax.experimental import pallas as pl
from jax.experimental.pallas import tpu as pltpu
from jax.sharding import PartitionSpec as P

SWEEPS = 8
ALPHA = 0.05
TIME_STEP = 0.5
WINDOW = 16
DECAY = ALPHA ** (1.0 / WINDOW)
NZ, NY, NX = 32, 128, 256
OWN = NX // WINDOW
WIDE = OWN + 16
SLAB = 2
CHIP = 4
CHIPS = NZ // CHIP
FIRST = 3
EXTRA = 16
REACH = 10
NARROW = OWN + 8
GROUPS = 2
EACH = 2
REALS = 4


def time_scale(n):
    return DECAY**n


def shift_rows():
    rows = []
    for p in range(8):
        angle = 2.0 * math.pi * p / WINDOW
        real = (1.0 - DECAY * math.cos(angle)) / TIME_STEP
        imag = DECAY * math.sin(angle) / TIME_STEP
        other = real if p else (1.0 + DECAY) / TIME_STEP
        rows.append((real, other, imag if p else 0.0))
    return rows


def spectrum_of(times):
    even = [times[j] + times[j + 8] for j in range(8)]
    odd = [times[j] - times[j + 8] for j in range(8)]
    f = [even[j] + even[j + 4] for j in range(4)]
    g = [even[j] - even[j + 4] for j in range(4)]
    parts = [None] * 16
    parts[0] = (f[0] + f[2]) + (f[1] + f[3])
    parts[8] = (f[0] + f[2]) - (f[1] + f[3])
    parts[4] = f[0] - f[2]
    parts[12] = f[3] - f[1]
    root = math.sqrt(0.5)
    less, more = (g[1] - g[3]) * root, (g[1] + g[3]) * root
    parts[2] = g[0] + less
    parts[6] = g[0] - less
    parts[10] = -(g[2] + more)
    parts[14] = g[2] - more
    less = [odd[j] - odd[8 - j] for j in range(1, 4)]
    more = [odd[j] + odd[8 - j] for j in range(1, 4)]
    for k in (1, 3, 5, 7):
        angle = math.pi * k / 8
        parts[k] = odd[0] + sum(math.cos(angle * (j + 1)) * less[j] for j in range(3))
        tail = sum(math.sin(angle * (j + 1)) * more[j] for j in range(3))
        parts[8 + k] = -(tail + odd[4]) if k % 4 == 1 else odd[4] - tail
    return parts


def times_of(parts):
    plus, minus = parts[0] + parts[8], parts[0] - parts[8]
    two = [None if j in (0, 8) else 2.0 * parts[j] for j in range(16)]
    f = [plus + two[4], minus - two[12], plus - two[4], minus + two[12]]
    root = math.sqrt(0.5)
    g = [
        two[2] + two[6],
        root * ((two[2] - two[10]) - (two[6] + two[14])),
        two[14] - two[10],
        root * ((two[6] - two[14]) - (two[2] + two[10])),
    ]
    even = [f[j] + g[j] for j in range(4)] + [f[j] - g[j] for j in range(4)]
    odd = [None] * 8
    odd[0] = (two[1] + two[3]) + (two[5] + two[7])
    odd[4] = (two[11] + two[15]) - (two[9] + two[13])
    for n in range(1, 4):
        c = sum(math.cos(math.pi * p * n / 8) * two[p] for p in (1, 3, 5, 7))
        s = sum(math.sin(math.pi * p * n / 8) * two[8 + p] for p in (1, 3, 5, 7))
        odd[n] = c - s
        odd[8 - n] = -(c + s)
    return [even[n] + odd[n] for n in range(8)] + [even[n] - odd[n] for n in range(8)]


def run_copies(pairs, sems):
    copies = [pltpu.make_async_copy(source, target, sems.at[i]) for i, (source, target) in enumerate(pairs)]
    for copy in copies:
        copy.start()
    return copies


def entry_kernel(iterate, kappa, velocity, outer, inner, out, held, turned, sems):
    step = lax.axis_index("tm")
    parity = lax.axis_index("space") % 2
    pairs = [(kappa, held.at[0])]
    pairs += [(velocity.at[d], held.at[1 + d]) for d in range(3)]
    pairs += [
        (iterate.at[0, parity], outer.at[0]),
        (kappa.at[parity], outer.at[1]),
        (iterate.at[0, 1 - parity], inner.at[0]),
        (kappa.at[1 - parity], inner.at[1]),
    ]
    copies = run_copies(pairs, sems)
    edge = jnp.zeros((8, NY), jnp.float32)
    for field in range(4):
        copies[field].wait()
        for plane in range(SLAB):
            spot = turned.at[SLAB * field + plane]
            spot[0:8] = edge
            spot[8 : 8 + NX] = held[field, plane].T
            spot[8 + NX : 16 + NX] = edge
            out[field, plane] = spot[pl.ds(pl.multiple_of(step * OWN, OWN), WIDE), :]
    for copy in copies[4:]:
        copy.wait()


def inside_kernel(forcing_hbm, iterate_hbm, kappa_hbm, velocity_hbm, base, rim, *scratch):
    forcing, iterate, kappa, velocity, sems = scratch
    pairs = [(kappa_hbm, kappa), (iterate_hbm, iterate), (velocity_hbm, velocity), (forcing_hbm, forcing)]
    for copy in run_copies(pairs, sems):
        copy.wait()
    row = lax.broadcasted_iota(jnp.int32, (NY, NX), 0)
    lane = lax.broadcasted_iota(jnp.int32, (NY, NX), 1)

    def shifted(array, dim, up):
        extent = NY if dim == 0 else NX
        index = row if dim == 0 else lane
        inside = index < extent - 1 if up else index > 0
        return jnp.where(inside, pltpu.roll(array, extent - 1 if up else 1, dim), 0.0)

    for plane in range(SLAB):
        centre, here = kappa[plane], iterate[0, plane]
        towards = -1.0 if plane == 0 else 1.0
        half = 0.5 * velocity[0, plane]
        face = 0.5 * (centre + kappa[1 - plane])
        diagonal = face + 0.5 * centre
        total = (face + towards * half) * iterate[0, 1 - plane]
        rim[plane] = 0.5 * centre - towards * half
        for dim in range(2):
            half = 0.5 * velocity[1 + dim, plane]
            for up, sign in ((True, -1.0), (False, 1.0)):
                face = 0.5 * (centre + shifted(centre, dim, up))
                diagonal += face
                total += (face + sign * half) * shifted(here, dim, up)
        base[plane] = forcing[0, plane] - here * (1.0 / TIME_STEP) - (diagonal * here - total)


def resid_kernel(base, rim, iterate, previous, outer, inner, out, turned):
    step = lax.axis_index("tm")
    place = lax.axis_index("space")
    even = place % 2 == 0
    leads = step % 4 == 0
    growth = jnp.exp(jnp.full((1, 1), step.astype(jnp.float32) / WINDOW * math.log(ALPHA), jnp.float32))
    edge = jnp.zeros((8, NY), jnp.float32)

    def turn(spot, array):
        spot[0:8] = edge
        spot[8 : 8 + NX] = array.T
        spot[8 + NX : 16 + NX] = edge

    carried = jnp.where(leads, 0.0, 1.0 / TIME_STEP)
    skip = jnp.where(leads, 0, 8)
    for plane in range(SLAB):
        side, other = (outer, inner) if plane == 0 else (inner, outer)
        ends = place == 0 if plane == 0 else place == 2 * CHIPS - 1
        here = iterate[0, plane]
        near = jnp.where(ends, 0.0, jnp.where(even, side[0], other[0]))
        far = jnp.where(ends, 0.0, 0.5 * jnp.where(even, side[1], other[1]))
        resid = base[plane] + previous[0, plane] * carried + (rim[plane] + far) * near - far * here
        turn(turned.at[plane], resid * growth)
        for c in range(WINDOW):
            out[c, WIDE * plane : WIDE * (plane + 1)] = turned[plane, OWN * c : OWN * c + WIDE]
        turn(turned.at[SLAB + plane], jnp.where(leads, previous[0, plane], here))
        for c in range(WINDOW):
            for number in range(2):
                start = pl.multiple_of(OWN * c + OWN * number + skip, 8)
                spot = SLAB * WIDE + EXTRA * plane + 8 * number
                out[c, spot : spot + 8] = turned[SLAB + plane, pl.ds(start, 8)]


def ahead_kernel(times, *outs):
    keeps, sends = outs[:GROUPS], outs[GROUPS:]
    core = lax.axis_index("space") % 2
    for plane in range(SLAB):
        for tile in range(WIDE // 8):
            rows = slice(8 * tile, 8 * tile + 8)
            values = [times[n, WIDE * plane + 8 * tile : WIDE * plane + 8 * tile + 8] for n in range(WINDOW)]
            spot = SLAB * WIDE + EXTRA * plane + 8 * (tile // 2)
            for n in (4, 8, 12):
                source = n - 1 if tile % 2 else n - 4
                values[n] += times[source, spot : spot + 8] * (time_scale(n) / TIME_STEP)
            parts = spectrum_of(values)
            for group, (keep, send) in enumerate(zip(keeps, sends)):
                for r in range(REALS):
                    index = 8 * (r // EACH) + EACH * group + r % EACH
                    low, high = parts[index], parts[index + 4]
                    keep[plane, r, rows] = jnp.where(core == 0, low, high)
                    send[REALS * plane + r, rows] = jnp.where(core == 0, high, low)


def pick(even, odd):
    return jnp.where(lax.axis_index("space") // 2 % 2 == 0, even, odd)


def gather_kernel(keep, got, chip, pair, other):
    core = lax.axis_index("space") % 2
    for r in range(REALS):
        values = []
        for plane in range(CHIP):
            mine, theirs = keep[plane % SLAB, r], got[REALS * (plane % SLAB) + r]
            values.append(jnp.where(core == plane // SLAB, mine, theirs))
            chip[plane, r] = values[plane]
        for plane in range(FIRST):
            pair[plane, r] = pick(values[plane + 1], values[plane])
            other[plane, r] = pick(values[plane], values[plane + 1])


def pack_kernel(pair, fields, other, out):
    for third, source in enumerate((pair, fields, other)):
        for field in range(4):
            for plane in range(SLAB):
                out[third, field, plane] = source[field, plane]


def back_kernel(*refs):
    mines, theirs, out = refs[:GROUPS], refs[GROUPS:-1], refs[-1]
    core = lax.axis_index("space") % 2
    for plane in range(SLAB):
        for tile in range(OWN // 8):
            rows = slice(8 * tile, 8 * tile + 8)
            parts = [None] * 16
            for group in range(GROUPS):
                for r in range(REALS):
                    index = 8 * (r // EACH) + EACH * group + r % EACH
                    one, two = mines[group][plane, r, rows], theirs[group][plane, r, rows]
                    parts[index] = jnp.where(core == 0, one, two)
                    parts[index + 4] = jnp.where(core == 0, two, one)
            values = times_of(parts)
            for n in range(WINDOW):
                out[n, plane, rows] = values[n] * (time_scale(-n) / WINDOW)


def update_kernel(correction, iterate, out):
    for plane in range(SLAB):
        turned = correction[:, plane].reshape(NX, NY).T
        out[0, plane] = iterate[0, plane] + turned


def prepare_kernel(pair, fields, other, got, cof, held):
    place = lax.axis_index("space")
    core, chip = place % 2, place // 2
    start = lax.axis_index("tm") * OWN - 8
    column = start + lax.broadcasted_iota(jnp.int32, (WIDE, NY), 0)
    lane = lax.broadcasted_iota(jnp.int32, (WIDE, NY), 1)
    rows = shift_rows()
    shifts = [[jnp.where(core == 0, rows[j][i], rows[4 + j][i]) for i in range(3)] for j in range(4)]
    for third in range(3):
        for field in range(4):
            for plane in range(SLAB):
                if third == 1:
                    value, partner = fields[field, plane], got[1, field, plane]
                else:
                    sources = [(pair[field, plane], got[0, field, plane]), (other[field, plane], got[2, field, plane])]
                    below, above = sources[::-1], sources
                    even, odd = below if third == 0 else above
                    value, partner = pick(even[0], odd[0]), pick(even[1], odd[1])
                    if field == 0:
                        outside = chip == (0 if third == 0 else CHIPS - 1)
                        value, partner = jnp.where(outside, 0.0, value), jnp.where(outside, 0.0, partner)
                held[field, CHIP * third + plane] = jnp.where(core == 0, value, partner)
                held[field, CHIP * third + SLAB + plane] = jnp.where(core == 0, partner, value)
    for z in range(REACH):
        spot = z + 1
        centre = held[0, spot]
        half = [0.5 * held[1 + d, spot] for d in range(3)]
        up_z = 0.5 * (centre + held[0, spot + 1])
        down_z = 0.5 * (centre + held[0, spot - 1])
        up_y = 0.5 * (centre + jnp.where(lane < NY - 1, pltpu.roll(centre, NY - 1, 1), 0.0))
        down_y = 0.5 * (centre + jnp.where(lane > 0, pltpu.roll(centre, 1, 1), 0.0))
        up_x = 0.5 * (centre + pltpu.roll(centre, WIDE - 1, 0))
        down_x = 0.5 * (centre + pltpu.roll(centre, 1, 0))
        diagonal = up_z + down_z + up_y + down_y + up_x + down_x
        plus_z, minus_z = up_z - half[0], down_z + half[0]
        if spot == 2 * CHIP - 1:
            plus_z = jnp.where(chip == CHIPS - 1, 0.0, plus_z)
        if spot == CHIP:
            minus_z = jnp.where(chip == 0, 0.0, minus_z)
        cof[z, 0] = plus_z
        cof[z, 1] = minus_z
        cof[z, 2] = jnp.where(lane < NY - 1, up_y - half[1], 0.0)
        cof[z, 3] = jnp.where(lane > 0, down_y + half[1], 0.0)
        cof[z, 4] = jnp.where(column < NX - 1, up_x - half[2], 0.0)
        cof[z, 5] = jnp.where(column > 0, down_x + half[2], 0.0)
        for j, (real, other, imag) in enumerate(shifts):
            den = real + diagonal
            scale = 1.0 / (den * den + imag * imag)
            cof[z, 6 + 2 * j] = den * scale
            cof[z, 7 + 2 * j] = -imag * scale
            if j == 0:
                den = other + diagonal
                cof[z, 14] = den / (den * den + imag * imag)


def divide(cof, z, j, total_real, total_imag):
    inv_real, inv_imag = cof[z, 6 + 2 * j], cof[z, 7 + 2 * j]
    inv_other = cof[z, 14] if j == 0 else inv_real
    return (
        total_real * inv_real - total_imag * inv_imag,
        total_real * inv_imag + total_imag * inv_other,
    )


def part_of(field, z, r, ahead=0):
    start = 8 + WIDE * (REALS * z + r) + ahead
    return field.at[start : start + WIDE]


def sweeps(group, cof, spec_of, src, dst, planes, shift, finish):
    for number, (first, end) in enumerate(planes):
        for z in range(first, end):
            here = z + shift
            for j in range(EACH):
                totals = []
                for r in (j, EACH + j):
                    centre = part_of(src, here, r)[...]
                    total = cof[z, 0] * part_of(src, here + 1, r)[...] + cof[z, 1] * part_of(src, here - 1, r)[...]
                    total += cof[z, 2] * pltpu.roll(centre, NY - 1, 1) + cof[z, 3] * pltpu.roll(centre, 1, 1)
                    total += cof[z, 4] * part_of(src, here, r, 1)[...] + cof[z, 5] * part_of(src, here, r, -1)[...]
                    totals.append(total + spec_of(z, r))
                for r, value in zip((j, EACH + j), divide(cof, z, EACH * group + j, *totals)):
                    if number == len(planes) - 1:
                        finish(z, r, value)
                    else:
                        part_of(dst, here, r)[...] = value
        src, dst = dst, src


def spectrum_reader(chip, pair, other):
    def spec_of(z, r):
        if z < FIRST:
            return pick(other[z, r], pair[z, r])
        if z < FIRST + CHIP:
            return chip[z - FIRST, r]
        return pick(pair[z - FIRST - CHIP, r], other[z - FIRST - CHIP, r])

    return spec_of


def first_kernel(group, chip, other, pair, cof, out, field_a, field_b):
    spec_of = spectrum_reader(chip, pair, other)
    for field in (field_a, field_b):
        field[0:8] = jnp.zeros((8, NY), jnp.float32)
        field[8 + WIDE * REALS * REACH :] = jnp.zeros((8, NY), jnp.float32)
    for z in range(REACH):
        for j in range(EACH):
            values = divide(cof, z, EACH * group + j, spec_of(z, j), spec_of(z, EACH + j))
            for r, value in zip((j, EACH + j), values):
                part_of(field_a, z, r)[...] = value

    def finish(z, r, value):
        out[z - FIRST, r] = value[4 : 4 + NARROW]

    sweeps(group, cof, spec_of, field_a, field_b, [(1, 9), (2, 8), (3, 7)], 0, finish)


def second_kernel(group, chip, other, pair, cof, own, other_own, pair_own, mine, theirs, field_a, field_b):
    core = lax.axis_index("space") % 2
    spec_of = spectrum_reader(chip, pair, other)
    for field in (field_a, field_b):
        field[0:8] = jnp.zeros((8, NY), jnp.float32)
        field[8 + WIDE * REALS * 3 * CHIP :] = jnp.zeros((8, NY), jnp.float32)
    edge = jnp.zeros((8, NY), jnp.float32)
    sources = ((other_own, pair_own), (own, own), (pair_own, other_own))
    for third, (even, odd) in enumerate(sources):
        for plane in range(CHIP):
            for r in range(REALS):
                spot = part_of(field_a, CHIP * third + plane, r)
                spot[0:8] = edge
                spot[WIDE - 8 : WIDE] = edge
                spot[4 : 4 + NARROW] = own[plane, r] if third == 1 else pick(even[plane, r], odd[plane, r])
    held = {}

    def finish(z, r, value):
        plane = z - FIRST
        value = value[8 : 8 + OWN]
        if plane < SLAB:
            held[plane, r] = value
        else:
            low_value = held.pop((plane - SLAB, r))
            mine[plane - SLAB, r] = jnp.where(core == 0, low_value, value)
            theirs[plane - SLAB, r] = jnp.where(core == 0, value, low_value)

    sweeps(group, cof, spec_of, field_a, field_b, [(0, 10), (1, 9), (2, 8), (3, 7)], 1, finish)


INSIDE_MIB = 53.25


def call(kernel, shapes, args, scratch=(), anywhere=False, mib=32):
    vmem = pl.BlockSpec(memory_space=pltpu.VMEM)
    several = isinstance(shapes, list)
    out_shape = [jax.ShapeDtypeStruct(shape, jnp.float32) for shape in (shapes if several else [shapes])]
    return pl.pallas_call(
        kernel,
        out_shape=out_shape if several else out_shape[0],
        in_specs=[pl.BlockSpec(memory_space=pl.ANY) if anywhere else vmem] * len(args),
        out_specs=[vmem] * len(shapes) if several else vmem,
        scratch_shapes=[pltpu.VMEM(dims, jnp.float32) if isinstance(dims, tuple) else dims for dims in scratch],
        compiler_params=pltpu.CompilerParams(vmem_limit_bytes=int(mib * 1024 * 1024)),
    )(*args)


def shards(forcing, iterate, kappa, velocity):
    block = (SLAB, NY, NX)
    cores = [(i, i ^ 1) for i in range(2 * CHIPS)]
    pairs = [(i, i ^ 2) for i in range(2 * CHIPS)]
    others = [(i, i + 2) for i in range(2 * CHIPS - 2) if i // 2 % 2]
    others += [(j, i) for i, j in others]
    others += [(i, i ^ 1) for i in (0, 1, 2 * CHIPS - 2, 2 * CHIPS - 1)]
    facing = [(i, (i + 1) % (2 * CHIPS)) for i in range(1, 2 * CHIPS, 2)]
    facing += [(j, i) for i, j in facing]
    previous = lax.ppermute(iterate, "tm", [(i, i // 4 * 4 + (i + 1) % 4) for i in range(WINDOW)])
    outer, inner, fields = call(
        entry_kernel,
        [block, block, (4, SLAB, WIDE, NY)],
        (iterate, kappa, velocity),
        [(4, *block), (8, NX + 16, NY), pltpu.SemaphoreType.DMA((8,))],
        anywhere=True,
        mib=53.25,
    )
    outer = lax.ppermute(outer, "space", facing)
    inner = lax.ppermute(inner, "space", cores)
    fields, inner = lax.optimization_barrier((fields, inner))
    fields_pair = lax.ppermute(fields, "space", pairs)
    fields_other = lax.ppermute(fields, "space", others)
    base, rim = call(
        inside_kernel,
        [block, block],
        (forcing, iterate, kappa, velocity),
        [(1, *block), (1, *block), block, (3, *block), pltpu.SemaphoreType.DMA((4,))],
        anywhere=True,
        mib=INSIDE_MIB,
    )
    outer, fields_pair, fields_other = lax.optimization_barrier((outer, fields_pair, fields_other))
    sent = call(
        resid_kernel,
        (WINDOW, SLAB * (WIDE + EXTRA), NY),
        (base, rim, iterate, previous, outer, inner),
        [(2 * SLAB, NX + 16, NY)],
    )
    times = lax.all_to_all(sent, "tm", 0, 0)
    parts = call(
        ahead_kernel,
        [(SLAB, REALS, WIDE, NY)] * GROUPS
        + [(SLAB * REALS, WIDE, NY)] * GROUPS,
        (times,),
    )
    got = [lax.ppermute(sent, "space", cores) for sent in parts[GROUPS:]]
    chips, pair_specs, other_specs = [], [], []
    for group in range(GROUPS):
        shape = (FIRST, REALS, WIDE, NY)
        chip, pair, other = call(gather_kernel, [(CHIP, REALS, WIDE, NY), shape, shape], (parts[group], got[group]))
        chips.append(chip)
        other_specs.append(lax.ppermute(other, "space", others))
        pair_specs.append(lax.ppermute(pair, "space", pairs))
    fields, chips[-1] = lax.optimization_barrier((fields, chips[-1]))
    held = call(pack_kernel, (3, 4, SLAB, WIDE, NY), (fields_pair, fields, fields_other))
    held = lax.ppermute(held, "space", cores)
    cof = call(
        prepare_kernel,
        (REACH, 15, WIDE, NY),
        (fields_pair, fields, fields_other, held),
        [(4, 3 * CHIP, WIDE, NY)],
    )
    owns, pair_owns, other_owns = [], [], []
    for group in range(GROUPS):
        own = call(
            functools.partial(first_kernel, group),
            (CHIP, REALS, NARROW, NY),
            (chips[group], other_specs[group], pair_specs[group], cof),
            [(16 + WIDE * REALS * REACH, NY)] * 2,
        )
        owns.append(own)
        other_owns.append(lax.ppermute(own, "space", others))
        pair_owns.append(lax.ppermute(own, "space", pairs))
    mines, theirs = [], []
    for group in range(GROUPS):
        mine, other = call(
            functools.partial(second_kernel, group),
            [(SLAB, REALS, OWN, NY)] * 2,
            (
                *(chips[group], other_specs[group], pair_specs[group], cof),
                *(owns[group], other_owns[group], pair_owns[group]),
            ),
            [(16 + WIDE * REALS * 3 * CHIP, NY)] * 2,
        )
        mines.append(mine)
        theirs.append(lax.ppermute(other, "space", cores))
    correction = call(back_kernel, (WINDOW, SLAB, OWN, NY), (*mines, *theirs))
    correction = lax.all_to_all(correction, "tm", 0, 0)
    return call(update_kernel, (1, SLAB, NY, NX), (correction, iterate))


def solution(mesh):
    in_specs = (
        P("tm", "space", None, None),
        P("tm", "space", None, None),
        P("space", None, None),
        P(None, "space", None, None),
    )
    out_specs = P("tm", "space", None, None)
    return jax.shard_map(shards, mesh=mesh, in_specs=in_specs, out_specs=out_specs, check_vma=False)
```

```python
import functools
import math

import jax
import jax.numpy as jnp
from jax import lax
from jax.experimental import pallas as pl
from jax.experimental.pallas import tpu as pltpu
from jax.sharding import PartitionSpec as P

SWEEPS = 8
ALPHA = 0.05
TIME_STEP = 0.5
WINDOW = 16
DECAY = ALPHA ** (1.0 / WINDOW)
NZ, NY, NX = 32, 128, 256
OWN = NX // WINDOW
WIDE = OWN + 16
SLAB = 2
CHIP = 4
CHIPS = NZ // CHIP
FIRST = 3
EXTRA = 16
REACH = 10
NARROW = OWN + 8
GROUPS = 2
EACH = 2
REALS = 4


def time_scale(n):
    return DECAY**n


def shift_rows():
    rows = []
    for p in range(8):
        angle = 2.0 * math.pi * p / WINDOW
        real = (1.0 - DECAY * math.cos(angle)) / TIME_STEP
        imag = DECAY * math.sin(angle) / TIME_STEP
        other = real if p else (1.0 + DECAY) / TIME_STEP
        rows.append((real, other, imag if p else 0.0))
    return rows


def spectrum_of(times):
    even = [times[j] + times[j + 8] for j in range(8)]
    odd = [times[j] - times[j + 8] for j in range(8)]
    f = [even[j] + even[j + 4] for j in range(4)]
    g = [even[j] - even[j + 4] for j in range(4)]
    parts = [None] * 16
    parts[0] = (f[0] + f[2]) + (f[1] + f[3])
    parts[8] = (f[0] + f[2]) - (f[1] + f[3])
    parts[4] = f[0] - f[2]
    parts[12] = f[3] - f[1]
    root = math.sqrt(0.5)
    less, more = (g[1] - g[3]) * root, (g[1] + g[3]) * root
    parts[2] = g[0] + less
    parts[6] = g[0] - less
    parts[10] = -(g[2] + more)
    parts[14] = g[2] - more
    less = [odd[j] - odd[8 - j] for j in range(1, 4)]
    more = [odd[j] + odd[8 - j] for j in range(1, 4)]
    for k in (1, 3, 5, 7):
        angle = math.pi * k / 8
        parts[k] = odd[0] + sum(math.cos(angle * (j + 1)) * less[j] for j in range(3))
        tail = sum(math.sin(angle * (j + 1)) * more[j] for j in range(3))
        parts[8 + k] = -(tail + odd[4]) if k % 4 == 1 else odd[4] - tail
    return parts


def times_of(parts):
    plus, minus = parts[0] + parts[8], parts[0] - parts[8]
    two = [None if j in (0, 8) else 2.0 * parts[j] for j in range(16)]
    f = [plus + two[4], minus - two[12], plus - two[4], minus + two[12]]
    root = math.sqrt(0.5)
    g = [
        two[2] + two[6],
        root * ((two[2] - two[10]) - (two[6] + two[14])),
        two[14] - two[10],
        root * ((two[6] - two[14]) - (two[2] + two[10])),
    ]
    even = [f[j] + g[j] for j in range(4)] + [f[j] - g[j] for j in range(4)]
    odd = [None] * 8
    odd[0] = (two[1] + two[3]) + (two[5] + two[7])
    odd[4] = (two[11] + two[15]) - (two[9] + two[13])
    for n in range(1, 4):
        c = sum(math.cos(math.pi * p * n / 8) * two[p] for p in (1, 3, 5, 7))
        s = sum(math.sin(math.pi * p * n / 8) * two[8 + p] for p in (1, 3, 5, 7))
        odd[n] = c - s
        odd[8 - n] = -(c + s)
    return [even[n] + odd[n] for n in range(8)] + [even[n] - odd[n] for n in range(8)]


def run_copies(pairs, sems):
    copies = [pltpu.make_async_copy(source, target, sems.at[i]) for i, (source, target) in enumerate(pairs)]
    for copy in copies:
        copy.start()
    return copies


def entry_kernel(iterate, kappa, velocity, first, second, outer, inner, out, held, turned, sems):
    step = lax.axis_index("tm")
    parity = lax.axis_index("space") % 2
    pairs = [(kappa, held.at[0])]
    pairs += [(velocity.at[d], held.at[1 + d]) for d in range(3)]
    pairs += [
        (iterate.at[0, 0], first),
        (iterate.at[0, 1], second),
        (iterate.at[0, parity], outer.at[0]),
        (kappa.at[parity], outer.at[1]),
        (iterate.at[0, 1 - parity], inner.at[0]),
        (kappa.at[1 - parity], inner.at[1]),
    ]
    copies = run_copies(pairs, sems)
    edge = jnp.zeros((8, NY), jnp.float32)
    for field in range(4):
        copies[field].wait()
        for plane in range(SLAB):
            spot = turned.at[SLAB * field + plane]
            spot[0:8] = edge
            spot[8 : 8 + NX] = held[field, plane].T
            spot[8 + NX : 16 + NX] = edge
            out[field, plane] = spot[pl.ds(pl.multiple_of(step * OWN, OWN), WIDE), :]
    for copy in copies[4:]:
        copy.wait()


def inside_kernel(forcing_hbm, iterate_hbm, kappa_hbm, velocity_hbm, base, rim, *scratch):
    forcing, iterate, kappa, velocity, sems = scratch
    pairs = [(kappa_hbm, kappa), (iterate_hbm, iterate), (velocity_hbm, velocity), (forcing_hbm, forcing)]
    for copy in run_copies(pairs, sems):
        copy.wait()
    row = lax.broadcasted_iota(jnp.int32, (NY, NX), 0)
    lane = lax.broadcasted_iota(jnp.int32, (NY, NX), 1)

    def shifted(array, dim, up):
        extent = NY if dim == 0 else NX
        index = row if dim == 0 else lane
        inside = index < extent - 1 if up else index > 0
        return jnp.where(inside, pltpu.roll(array, extent - 1 if up else 1, dim), 0.0)

    for plane in range(SLAB):
        centre, here = kappa[plane], iterate[0, plane]
        towards = -1.0 if plane == 0 else 1.0
        half = 0.5 * velocity[0, plane]
        face = 0.5 * (centre + kappa[1 - plane])
        diagonal = face + 0.5 * centre
        total = (face + towards * half) * iterate[0, 1 - plane]
        rim[plane] = 0.5 * centre - towards * half
        for dim in range(2):
            half = 0.5 * velocity[1 + dim, plane]
            for up, sign in ((True, -1.0), (False, 1.0)):
                face = 0.5 * (centre + shifted(centre, dim, up))
                diagonal += face
                total += (face + sign * half) * shifted(here, dim, up)
        base[plane] = forcing[0, plane] - here * (1.0 / TIME_STEP) - (diagonal * here - total)


def resid_kernel(base, rim, iterate, first, second, outer, inner, out, turned):
    step = lax.axis_index("tm")
    place = lax.axis_index("space")
    even = place % 2 == 0
    leads = step % 4 == 0
    growth = jnp.exp(jnp.full((1, 1), step.astype(jnp.float32) / WINDOW * math.log(ALPHA), jnp.float32))
    edge = jnp.zeros((8, NY), jnp.float32)

    def turn(spot, array):
        spot[0:8] = edge
        spot[8 : 8 + NX] = array.T
        spot[8 + NX : 16 + NX] = edge

    before = (first, second)
    skip = jnp.where(leads, 0, 8)
    for plane in range(SLAB):
        side, other = (outer, inner) if plane == 0 else (inner, outer)
        ends = place == 0 if plane == 0 else place == 2 * CHIPS - 1
        here = iterate[0, plane]
        near = jnp.where(ends, 0.0, jnp.where(even, side[0], other[0]))
        far = jnp.where(ends, 0.0, 0.5 * jnp.where(even, side[1], other[1]))
        carried = jnp.where(step == 0 if plane == 0 else leads, 0.0, 1.0 / TIME_STEP)
        resid = base[plane] + before[plane][...] * carried + (rim[plane] + far) * near - far * here
        turn(turned.at[plane], resid * growth)
        for c in range(WINDOW):
            out[c, WIDE * plane : WIDE * (plane + 1)] = turned[plane, OWN * c : OWN * c + WIDE]
    turn(turned.at[SLAB], jnp.where(leads, second[...], iterate[0, 1]))
    for c in range(WINDOW):
        for number in range(2):
            start = pl.multiple_of(OWN * c + OWN * number + skip, 8)
            spot = SLAB * WIDE + 8 * number
            out[c, spot : spot + 8] = turned[SLAB, pl.ds(start, 8)]


def ahead_kernel(times, *outs):
    keeps, sends = outs[:GROUPS], outs[GROUPS:]
    core = lax.axis_index("space") % 2
    for plane in range(SLAB):
        for tile in range(WIDE // 8):
            rows = slice(8 * tile, 8 * tile + 8)
            values = [times[n, WIDE * plane + 8 * tile : WIDE * plane + 8 * tile + 8] for n in range(WINDOW)]
            spot = SLAB * WIDE + 8 * (tile // 2)
            for n in (4, 8, 12) if plane == 1 else ():
                source = n - 1 if tile % 2 else n - 4
                values[n] += times[source, spot : spot + 8] * (time_scale(n) / TIME_STEP)
            parts = spectrum_of(values)
            for group, (keep, send) in enumerate(zip(keeps, sends)):
                for r in range(REALS):
                    index = 8 * (r // EACH) + EACH * group + r % EACH
                    low, high = parts[index], parts[index + 4]
                    keep[plane, r, rows] = jnp.where(core == 0, low, high)
                    send[REALS * plane + r, rows] = jnp.where(core == 0, high, low)


def pick(even, odd):
    return jnp.where(lax.axis_index("space") // 2 % 2 == 0, even, odd)


def gather_kernel(keep, got, chip, pair, other):
    core = lax.axis_index("space") % 2
    for r in range(REALS):
        values = []
        for plane in range(CHIP):
            mine, theirs = keep[plane % SLAB, r], got[REALS * (plane % SLAB) + r]
            values.append(jnp.where(core == plane // SLAB, mine, theirs))
            chip[plane, r] = values[plane]
        for plane in range(FIRST):
            pair[plane, r] = pick(values[plane + 1], values[plane])
            other[plane, r] = pick(values[plane], values[plane + 1])


def pack_kernel(pair, fields, other, out):
    for third, source in enumerate((pair, fields, other)):
        for field in range(4):
            for plane in range(SLAB):
                out[third, field, plane] = source[field, plane]


def back_kernel(*refs):
    mines, theirs, out = refs[:GROUPS], refs[GROUPS:-1], refs[-1]
    core = lax.axis_index("space") % 2
    for plane in range(SLAB):
        for tile in range(OWN // 8):
            rows = slice(8 * tile, 8 * tile + 8)
            parts = [None] * 16
            for group in range(GROUPS):
                for r in range(REALS):
                    index = 8 * (r // EACH) + EACH * group + r % EACH
                    one, two = mines[group][plane, r, rows], theirs[group][plane, r, rows]
                    parts[index] = jnp.where(core == 0, one, two)
                    parts[index + 4] = jnp.where(core == 0, two, one)
            values = times_of(parts)
            for n in range(WINDOW):
                out[n, plane, rows] = values[n] * (time_scale(-n) / WINDOW)


def update_kernel(correction, iterate, out):
    for plane in range(SLAB):
        turned = correction[:, plane].reshape(NX, NY).T
        out[0, plane] = iterate[0, plane] + turned


def prepare_kernel(pair, fields, other, got, cof, held):
    place = lax.axis_index("space")
    core, chip = place % 2, place // 2
    start = lax.axis_index("tm") * OWN - 8
    column = start + lax.broadcasted_iota(jnp.int32, (WIDE, NY), 0)
    lane = lax.broadcasted_iota(jnp.int32, (WIDE, NY), 1)
    rows = shift_rows()
    shifts = [[jnp.where(core == 0, rows[j][i], rows[4 + j][i]) for i in range(3)] for j in range(4)]
    for third in range(3):
        for field in range(4):
            for plane in range(SLAB):
                if third == 1:
                    value, partner = fields[field, plane], got[1, field, plane]
                else:
                    sources = [(pair[field, plane], got[0, field, plane]), (other[field, plane], got[2, field, plane])]
                    below, above = sources[::-1], sources
                    even, odd = below if third == 0 else above
                    value, partner = pick(even[0], odd[0]), pick(even[1], odd[1])
                    if field == 0:
                        outside = chip == (0 if third == 0 else CHIPS - 1)
                        value, partner = jnp.where(outside, 0.0, value), jnp.where(outside, 0.0, partner)
                held[field, CHIP * third + plane] = jnp.where(core == 0, value, partner)
                held[field, CHIP * third + SLAB + plane] = jnp.where(core == 0, partner, value)
    for z in range(REACH):
        spot = z + 1
        centre = held[0, spot]
        half = [0.5 * held[1 + d, spot] for d in range(3)]
        up_z = 0.5 * (centre + held[0, spot + 1])
        down_z = 0.5 * (centre + held[0, spot - 1])
        up_y = 0.5 * (centre + jnp.where(lane < NY - 1, pltpu.roll(centre, NY - 1, 1), 0.0))
        down_y = 0.5 * (centre + jnp.where(lane > 0, pltpu.roll(centre, 1, 1), 0.0))
        up_x = 0.5 * (centre + pltpu.roll(centre, WIDE - 1, 0))
        down_x = 0.5 * (centre + pltpu.roll(centre, 1, 0))
        diagonal = up_z + down_z + up_y + down_y + up_x + down_x
        plus_z, minus_z = up_z - half[0], down_z + half[0]
        if spot == 2 * CHIP - 1:
            plus_z = jnp.where(chip == CHIPS - 1, 0.0, plus_z)
        if spot == CHIP:
            minus_z = jnp.where(chip == 0, 0.0, minus_z)
        cof[z, 0] = plus_z
        cof[z, 1] = minus_z
        cof[z, 2] = jnp.where(lane < NY - 1, up_y - half[1], 0.0)
        cof[z, 3] = jnp.where(lane > 0, down_y + half[1], 0.0)
        cof[z, 4] = jnp.where(column < NX - 1, up_x - half[2], 0.0)
        cof[z, 5] = jnp.where(column > 0, down_x + half[2], 0.0)
        for j, (real, other, imag) in enumerate(shifts):
            den = real + diagonal
            scale = 1.0 / (den * den + imag * imag)
            cof[z, 6 + 2 * j] = den * scale
            cof[z, 7 + 2 * j] = -imag * scale
            if j == 0:
                den = other + diagonal
                cof[z, 14] = den / (den * den + imag * imag)


def divide(cof, z, j, total_real, total_imag):
    inv_real, inv_imag = cof[z, 6 + 2 * j], cof[z, 7 + 2 * j]
    inv_other = cof[z, 14] if j == 0 else inv_real
    return (
        total_real * inv_real - total_imag * inv_imag,
        total_real * inv_imag + total_imag * inv_other,
    )


def part_of(field, z, r, ahead=0):
    start = 8 + WIDE * (REALS * z + r) + ahead
    return field.at[start : start + WIDE]


def sweeps(group, cof, spec_of, src, dst, planes, shift, finish):
    for number, (first, end) in enumerate(planes):
        for z in range(first, end):
            here = z + shift
            for j in range(EACH):
                totals = []
                for r in (j, EACH + j):
                    centre = part_of(src, here, r)[...]
                    total = cof[z, 0] * part_of(src, here + 1, r)[...] + cof[z, 1] * part_of(src, here - 1, r)[...]
                    total += cof[z, 2] * pltpu.roll(centre, NY - 1, 1) + cof[z, 3] * pltpu.roll(centre, 1, 1)
                    total += cof[z, 4] * part_of(src, here, r, 1)[...] + cof[z, 5] * part_of(src, here, r, -1)[...]
                    totals.append(total + spec_of(z, r))
                for r, value in zip((j, EACH + j), divide(cof, z, EACH * group + j, *totals)):
                    if number == len(planes) - 1:
                        finish(z, r, value)
                    else:
                        part_of(dst, here, r)[...] = value
        src, dst = dst, src


def spectrum_reader(chip, pair, other):
    def spec_of(z, r):
        if z < FIRST:
            return pick(other[z, r], pair[z, r])
        if z < FIRST + CHIP:
            return chip[z - FIRST, r]
        return pick(pair[z - FIRST - CHIP, r], other[z - FIRST - CHIP, r])

    return spec_of


def first_kernel(group, chip, other, pair, cof, out, field_a, field_b):
    spec_of = spectrum_reader(chip, pair, other)
    for field in (field_a, field_b):
        field[0:8] = jnp.zeros((8, NY), jnp.float32)
        field[8 + WIDE * REALS * REACH :] = jnp.zeros((8, NY), jnp.float32)
    for z in range(REACH):
        for j in range(EACH):
            values = divide(cof, z, EACH * group + j, spec_of(z, j), spec_of(z, EACH + j))
            for r, value in zip((j, EACH + j), values):
                part_of(field_a, z, r)[...] = value

    def finish(z, r, value):
        out[z - FIRST, r] = value[4 : 4 + NARROW]

    sweeps(group, cof, spec_of, field_a, field_b, [(1, 9), (2, 8), (3, 7)], 0, finish)


def second_kernel(group, chip, other, pair, cof, own, other_own, pair_own, mine, theirs, field_a, field_b):
    core = lax.axis_index("space") % 2
    spec_of = spectrum_reader(chip, pair, other)
    for field in (field_a, field_b):
        field[0:8] = jnp.zeros((8, NY), jnp.float32)
        field[8 + WIDE * REALS * 3 * CHIP :] = jnp.zeros((8, NY), jnp.float32)
    edge = jnp.zeros((8, NY), jnp.float32)
    sources = ((other_own, pair_own), (own, own), (pair_own, other_own))
    for third, (even, odd) in enumerate(sources):
        for plane in range(CHIP):
            for r in range(REALS):
                spot = part_of(field_a, CHIP * third + plane, r)
                spot[0:8] = edge
                spot[WIDE - 8 : WIDE] = edge
                spot[4 : 4 + NARROW] = own[plane, r] if third == 1 else pick(even[plane, r], odd[plane, r])
    held = {}

    def finish(z, r, value):
        plane = z - FIRST
        value = value[8 : 8 + OWN]
        if plane < SLAB:
            held[plane, r] = value
        else:
            low_value = held.pop((plane - SLAB, r))
            mine[plane - SLAB, r] = jnp.where(core == 0, low_value, value)
            theirs[plane - SLAB, r] = jnp.where(core == 0, value, low_value)

    sweeps(group, cof, spec_of, field_a, field_b, [(0, 10), (1, 9), (2, 8), (3, 7)], 1, finish)


INSIDE_MIB = 53.25


def call(kernel, shapes, args, scratch=(), anywhere=False, mib=32):
    vmem = pl.BlockSpec(memory_space=pltpu.VMEM)
    several = isinstance(shapes, list)
    out_shape = [jax.ShapeDtypeStruct(shape, jnp.float32) for shape in (shapes if several else [shapes])]
    return pl.pallas_call(
        kernel,
        out_shape=out_shape if several else out_shape[0],
        in_specs=[pl.BlockSpec(memory_space=pl.ANY) if anywhere else vmem] * len(args),
        out_specs=[vmem] * len(shapes) if several else vmem,
        scratch_shapes=[pltpu.VMEM(dims, jnp.float32) if isinstance(dims, tuple) else dims for dims in scratch],
        compiler_params=pltpu.CompilerParams(vmem_limit_bytes=int(mib * 1024 * 1024)),
    )(*args)


def shards(forcing, iterate, kappa, velocity):
    block = (SLAB, NY, NX)
    cores = [(i, i ^ 1) for i in range(2 * CHIPS)]
    pairs = [(i, i ^ 2) for i in range(2 * CHIPS)]
    others = [(i, i + 2) for i in range(2 * CHIPS - 2) if i // 2 % 2]
    others += [(j, i) for i, j in others]
    others += [(i, i ^ 1) for i in (0, 1, 2 * CHIPS - 2, 2 * CHIPS - 1)]
    facing = [(i, (i + 1) % (2 * CHIPS)) for i in range(1, 2 * CHIPS, 2)]
    facing += [(j, i) for i, j in facing]
    first, second, outer, inner, fields = call(
        entry_kernel,
        [(NY, NX), (NY, NX), block, block, (4, SLAB, WIDE, NY)],
        (iterate, kappa, velocity),
        [(4, *block), (8, NX + 16, NY), pltpu.SemaphoreType.DMA((10,))],
        anywhere=True,
        mib=53,
    )
    first = lax.ppermute(first, "tm", [(i, (i + 1) % WINDOW) for i in range(WINDOW)])
    second = lax.ppermute(second, "tm", [(i, i // 4 * 4 + (i + 1) % 4) for i in range(WINDOW)])
    outer = lax.ppermute(outer, "space", facing)
    inner = lax.ppermute(inner, "space", cores)
    fields, inner = lax.optimization_barrier((fields, inner))
    fields_pair = lax.ppermute(fields, "space", pairs)
    fields_other = lax.ppermute(fields, "space", others)
    base, rim = call(
        inside_kernel,
        [block, block],
        (forcing, iterate, kappa, velocity),
        [(1, *block), (1, *block), block, (3, *block), pltpu.SemaphoreType.DMA((4,))],
        anywhere=True,
        mib=INSIDE_MIB,
    )
    outer, fields_pair, fields_other = lax.optimization_barrier((outer, fields_pair, fields_other))
    sent = call(
        resid_kernel,
        (WINDOW, SLAB * WIDE + EXTRA, NY),
        (base, rim, iterate, first, second, outer, inner),
        [(SLAB + 1, NX + 16, NY)],
    )
    times = lax.all_to_all(sent, "tm", 0, 0)
    parts = call(
        ahead_kernel,
        [(SLAB, REALS, WIDE, NY)] * GROUPS
        + [(SLAB * REALS, WIDE, NY)] * GROUPS,
        (times,),
    )
    got = [lax.ppermute(sent, "space", cores) for sent in parts[GROUPS:]]
    chips, pair_specs, other_specs = [], [], []
    for group in range(GROUPS):
        shape = (FIRST, REALS, WIDE, NY)
        chip, pair, other = call(gather_kernel, [(CHIP, REALS, WIDE, NY), shape, shape], (parts[group], got[group]))
        chips.append(chip)
        other_specs.append(lax.ppermute(other, "space", others))
        pair_specs.append(lax.ppermute(pair, "space", pairs))
    fields, chips[-1] = lax.optimization_barrier((fields, chips[-1]))
    held = call(pack_kernel, (3, 4, SLAB, WIDE, NY), (fields_pair, fields, fields_other))
    held = lax.ppermute(held, "space", cores)
    cof = call(
        prepare_kernel,
        (REACH, 15, WIDE, NY),
        (fields_pair, fields, fields_other, held),
        [(4, 3 * CHIP, WIDE, NY)],
    )
    owns, pair_owns, other_owns = [], [], []
    for group in range(GROUPS):
        own = call(
            functools.partial(first_kernel, group),
            (CHIP, REALS, NARROW, NY),
            (chips[group], other_specs[group], pair_specs[group], cof),
            [(16 + WIDE * REALS * REACH, NY)] * 2,
        )
        owns.append(own)
        other_owns.append(lax.ppermute(own, "space", others))
        pair_owns.append(lax.ppermute(own, "space", pairs))
    mines, theirs = [], []
    for group in range(GROUPS):
        mine, other = call(
            functools.partial(second_kernel, group),
            [(SLAB, REALS, OWN, NY)] * 2,
            (
                *(chips[group], other_specs[group], pair_specs[group], cof),
                *(owns[group], other_owns[group], pair_owns[group]),
            ),
            [(16 + WIDE * REALS * 3 * CHIP, NY)] * 2,
        )
        mines.append(mine)
        theirs.append(lax.ppermute(other, "space", cores))
    correction = call(back_kernel, (WINDOW, SLAB, OWN, NY), (*mines, *theirs))
    correction = lax.all_to_all(correction, "tm", 0, 0)
    return call(update_kernel, (1, SLAB, NY, NX), (correction, iterate))


def solution(mesh):
    in_specs = (
        P("tm", "space", None, None),
        P("tm", "space", None, None),
        P("space", None, None),
        P(None, "space", None, None),
    )
    out_specs = P("tm", "space", None, None)
    return jax.shard_map(shards, mesh=mesh, in_specs=in_specs, out_specs=out_specs, check_vma=False)
```

```python
import functools
import math

import jax
import jax.numpy as jnp
from jax import lax
from jax.experimental import pallas as pl
from jax.experimental.pallas import tpu as pltpu
from jax.sharding import PartitionSpec as P

SWEEPS = 8
ALPHA = 0.05
TIME_STEP = 0.5
WINDOW = 16
DECAY = ALPHA ** (1.0 / WINDOW)
NZ, NY, NX = 32, 128, 256
OWN = NX // WINDOW
WIDE = OWN + 16
SLAB = 2
CHIP = 4
CHIPS = NZ // CHIP
FIRST = 3
EXTRA = 16
REACH = 10
NARROW = OWN + 8
GROUPS = 2
EACH = 2
REALS = 4


def time_scale(n):
    return DECAY**n


def shift_rows():
    rows = []
    for p in range(8):
        angle = 2.0 * math.pi * p / WINDOW
        real = (1.0 - DECAY * math.cos(angle)) / TIME_STEP
        imag = DECAY * math.sin(angle) / TIME_STEP
        other = real if p else (1.0 + DECAY) / TIME_STEP
        rows.append((real, other, imag if p else 0.0))
    return rows


def spectrum_of(times):
    even = [times[j] + times[j + 8] for j in range(8)]
    odd = [times[j] - times[j + 8] for j in range(8)]
    f = [even[j] + even[j + 4] for j in range(4)]
    g = [even[j] - even[j + 4] for j in range(4)]
    parts = [None] * 16
    parts[0] = (f[0] + f[2]) + (f[1] + f[3])
    parts[8] = (f[0] + f[2]) - (f[1] + f[3])
    parts[4] = f[0] - f[2]
    parts[12] = f[3] - f[1]
    root = math.sqrt(0.5)
    less, more = (g[1] - g[3]) * root, (g[1] + g[3]) * root
    parts[2] = g[0] + less
    parts[6] = g[0] - less
    parts[10] = -(g[2] + more)
    parts[14] = g[2] - more
    less = [odd[j] - odd[8 - j] for j in range(1, 4)]
    more = [odd[j] + odd[8 - j] for j in range(1, 4)]
    for k in (1, 3, 5, 7):
        angle = math.pi * k / 8
        parts[k] = odd[0] + sum(math.cos(angle * (j + 1)) * less[j] for j in range(3))
        tail = sum(math.sin(angle * (j + 1)) * more[j] for j in range(3))
        parts[8 + k] = -(tail + odd[4]) if k % 4 == 1 else odd[4] - tail
    return parts


def times_of(parts):
    plus, minus = parts[0] + parts[8], parts[0] - parts[8]
    two = [None if j in (0, 8) else 2.0 * parts[j] for j in range(16)]
    f = [plus + two[4], minus - two[12], plus - two[4], minus + two[12]]
    root = math.sqrt(0.5)
    g = [
        two[2] + two[6],
        root * ((two[2] - two[10]) - (two[6] + two[14])),
        two[14] - two[10],
        root * ((two[6] - two[14]) - (two[2] + two[10])),
    ]
    even = [f[j] + g[j] for j in range(4)] + [f[j] - g[j] for j in range(4)]
    odd = [None] * 8
    odd[0] = (two[1] + two[3]) + (two[5] + two[7])
    odd[4] = (two[11] + two[15]) - (two[9] + two[13])
    for n in range(1, 4):
        c = sum(math.cos(math.pi * p * n / 8) * two[p] for p in (1, 3, 5, 7))
        s = sum(math.sin(math.pi * p * n / 8) * two[8 + p] for p in (1, 3, 5, 7))
        odd[n] = c - s
        odd[8 - n] = -(c + s)
    return [even[n] + odd[n] for n in range(8)] + [even[n] - odd[n] for n in range(8)]


def run_copies(pairs, sems):
    copies = [pltpu.make_async_copy(source, target, sems.at[i]) for i, (source, target) in enumerate(pairs)]
    for copy in copies:
        copy.start()
    return copies


def entry_kernel(iterate, kappa, velocity, first, second, outer, inner, out, held, turned, sems):
    step = lax.axis_index("tm")
    parity = lax.axis_index("space") % 2
    pairs = [(kappa, held.at[0])]
    pairs += [(velocity.at[d], held.at[1 + d]) for d in range(3)]
    pairs += [
        (iterate.at[0, 0], first),
        (iterate.at[0, 1], second),
        (iterate.at[0, parity], outer.at[0]),
        (kappa.at[parity], outer.at[1]),
        (iterate.at[0, 1 - parity], inner.at[0]),
        (kappa.at[1 - parity], inner.at[1]),
    ]
    copies = run_copies(pairs, sems)
    edge = jnp.zeros((8, NY), jnp.float32)
    for field in range(4):
        copies[field].wait()
        for plane in range(SLAB):
            spot = turned.at[SLAB * field + plane]
            spot[0:8] = edge
            spot[8 : 8 + NX] = held[field, plane].T
            spot[8 + NX : 16 + NX] = edge
            out[field, plane] = spot[pl.ds(pl.multiple_of(step * OWN, OWN), WIDE), :]
    for copy in copies[4:]:
        copy.wait()


def inside_kernel(forcing_hbm, iterate_hbm, kappa_hbm, velocity_hbm, base, rim, *scratch):
    forcing, iterate, kappa, velocity, sems = scratch
    pairs = [(kappa_hbm, kappa), (iterate_hbm, iterate), (velocity_hbm, velocity), (forcing_hbm, forcing)]
    for copy in run_copies(pairs, sems):
        copy.wait()
    row = lax.broadcasted_iota(jnp.int32, (NY, NX), 0)
    lane = lax.broadcasted_iota(jnp.int32, (NY, NX), 1)

    def shifted(array, dim, up):
        extent = NY if dim == 0 else NX
        index = row if dim == 0 else lane
        inside = index < extent - 1 if up else index > 0
        return jnp.where(inside, pltpu.roll(array, extent - 1 if up else 1, dim), 0.0)

    for plane in range(SLAB):
        centre, here = kappa[plane], iterate[0, plane]
        towards = -1.0 if plane == 0 else 1.0
        half = 0.5 * velocity[0, plane]
        face = 0.5 * (centre + kappa[1 - plane])
        diagonal = face + 0.5 * centre
        total = (face + towards * half) * iterate[0, 1 - plane]
        rim[plane] = 0.5 * centre - towards * half
        for dim in range(2):
            half = 0.5 * velocity[1 + dim, plane]
            for up, sign in ((True, -1.0), (False, 1.0)):
                face = 0.5 * (centre + shifted(centre, dim, up))
                diagonal += face
                total += (face + sign * half) * shifted(here, dim, up)
        base[plane] = forcing[0, plane] - here * (1.0 / TIME_STEP) - (diagonal * here - total)


def resid_kernel(base, rim, iterate, first, second, outer, inner, out, turned):
    step = lax.axis_index("tm")
    place = lax.axis_index("space")
    even = place % 2 == 0
    leads = step % 4 == 0
    growth = jnp.exp(jnp.full((1, 1), step.astype(jnp.float32) / WINDOW * math.log(ALPHA), jnp.float32))
    edge = jnp.zeros((8, NY), jnp.float32)

    def turn(spot, array):
        spot[0:8] = edge
        spot[8 : 8 + NX] = array.T
        spot[8 + NX : 16 + NX] = edge

    before = (first, second)
    skip = jnp.where(leads, 0, 8)
    for plane in range(SLAB):
        side, other = (outer, inner) if plane == 0 else (inner, outer)
        ends = place == 0 if plane == 0 else place == 2 * CHIPS - 1
        here = iterate[0, plane]
        near = jnp.where(ends, 0.0, jnp.where(even, side[0], other[0]))
        far = jnp.where(ends, 0.0, 0.5 * jnp.where(even, side[1], other[1]))
        carried = jnp.where(step == 0 if plane == 0 else leads, 0.0, 1.0 / TIME_STEP)
        resid = base[plane] + before[plane][...] * carried + (rim[plane] + far) * near - far * here
        turn(turned.at[plane], resid * growth)
        for c in range(WINDOW):
            out[c, WIDE * plane : WIDE * (plane + 1)] = turned[plane, OWN * c : OWN * c + WIDE]
    turn(turned.at[SLAB], jnp.where(leads, second[...], iterate[0, 1]))
    for c in range(WINDOW):
        for number in range(2):
            start = pl.multiple_of(OWN * c + OWN * number + skip, 8)
            spot = SLAB * WIDE + 8 * number
            out[c, spot : spot + 8] = turned[SLAB, pl.ds(start, 8)]


def ahead_kernel(times, *outs):
    keeps, sends = outs[:GROUPS], outs[GROUPS:]
    core = lax.axis_index("space") % 2
    for plane in range(SLAB):
        for tile in range(WIDE // 8):
            rows = slice(8 * tile, 8 * tile + 8)
            values = [times[n, WIDE * plane + 8 * tile : WIDE * plane + 8 * tile + 8] for n in range(WINDOW)]
            spot = SLAB * WIDE + 8 * (tile // 2)
            for n in (4, 8, 12) if plane == 1 else ():
                source = n - 1 if tile % 2 else n - 4
                values[n] += times[source, spot : spot + 8] * (time_scale(n) / TIME_STEP)
            parts = spectrum_of(values)
            for group, (keep, send) in enumerate(zip(keeps, sends)):
                for r in range(REALS):
                    index = 8 * (r // EACH) + EACH * group + r % EACH
                    low, high = parts[index], parts[index + 4]
                    keep[plane, r, rows] = jnp.where(core == 0, low, high)
                    send[REALS * plane + r, rows] = jnp.where(core == 0, high, low)


def pick(even, odd):
    return jnp.where(lax.axis_index("space") // 2 % 2 == 0, even, odd)


def gather_kernel(keep, got, chip, pair, other):
    core = lax.axis_index("space") % 2
    for r in range(REALS):
        values = []
        for plane in range(CHIP):
            mine, theirs = keep[plane % SLAB, r], got[REALS * (plane % SLAB) + r]
            values.append(jnp.where(core == plane // SLAB, mine, theirs))
            chip[plane, r] = values[plane]
        for plane in range(FIRST):
            pair[plane, r] = pick(values[plane + 1], values[plane])
            other[plane, r] = pick(values[plane], values[plane + 1])


def pack_kernel(pair, fields, other, out):
    for third, source in enumerate((pair, fields, other)):
        for field in range(4):
            for plane in range(SLAB):
                out[third, field, plane] = source[field, plane]


def back_kernel(*refs):
    mines, theirs, out = refs[:GROUPS], refs[GROUPS:-1], refs[-1]
    core = lax.axis_index("space") % 2
    for plane in range(SLAB):
        for tile in range(OWN // 8):
            rows = slice(8 * tile, 8 * tile + 8)
            parts = [None] * 16
            for group in range(GROUPS):
                for r in range(REALS):
                    index = 8 * (r // EACH) + EACH * group + r % EACH
                    one, two = mines[group][plane, r, rows], theirs[group][plane, r, rows]
                    parts[index] = jnp.where(core == 0, one, two)
                    parts[index + 4] = jnp.where(core == 0, two, one)
            values = times_of(parts)
            for n in range(WINDOW):
                out[n, plane, rows] = values[n] * (time_scale(-n) / WINDOW)


def update_kernel(correction, iterate, out):
    for plane in range(SLAB):
        turned = correction[:, plane].reshape(NX, NY).T
        out[0, plane] = iterate[0, plane] + turned


def prepare_kernel(pair, fields, other, got, cof, held):
    place = lax.axis_index("space")
    core, chip = place % 2, place // 2
    start = lax.axis_index("tm") * OWN - 8
    column = start + lax.broadcasted_iota(jnp.int32, (WIDE, NY), 0)
    lane = lax.broadcasted_iota(jnp.int32, (WIDE, NY), 1)
    rows = shift_rows()
    shifts = [[jnp.where(core == 0, rows[j][i], rows[4 + j][i]) for i in range(3)] for j in range(4)]
    for third in range(3):
        for field in range(4):
            for plane in range(SLAB):
                if third == 1:
                    value, partner = fields[field, plane], got[1, field, plane]
                else:
                    sources = [(pair[field, plane], got[0, field, plane]), (other[field, plane], got[2, field, plane])]
                    below, above = sources[::-1], sources
                    even, odd = below if third == 0 else above
                    value, partner = pick(even[0], odd[0]), pick(even[1], odd[1])
                    if field == 0:
                        outside = chip == (0 if third == 0 else CHIPS - 1)
                        value, partner = jnp.where(outside, 0.0, value), jnp.where(outside, 0.0, partner)
                held[field, CHIP * third + plane] = jnp.where(core == 0, value, partner)
                held[field, CHIP * third + SLAB + plane] = jnp.where(core == 0, partner, value)
    for z in range(REACH):
        spot = z + 1
        centre = held[0, spot]
        half = [0.5 * held[1 + d, spot] for d in range(3)]
        up_z = 0.5 * (centre + held[0, spot + 1])
        down_z = 0.5 * (centre + held[0, spot - 1])
        up_y = 0.5 * (centre + jnp.where(lane < NY - 1, pltpu.roll(centre, NY - 1, 1), 0.0))
        down_y = 0.5 * (centre + jnp.where(lane > 0, pltpu.roll(centre, 1, 1), 0.0))
        up_x = 0.5 * (centre + pltpu.roll(centre, WIDE - 1, 0))
        down_x = 0.5 * (centre + pltpu.roll(centre, 1, 0))
        diagonal = up_z + down_z + up_y + down_y + up_x + down_x
        plus_z, minus_z = up_z - half[0], down_z + half[0]
        if spot == 2 * CHIP - 1:
            plus_z = jnp.where(chip == CHIPS - 1, 0.0, plus_z)
        if spot == CHIP:
            minus_z = jnp.where(chip == 0, 0.0, minus_z)
        cof[z, 0] = plus_z
        cof[z, 1] = minus_z
        cof[z, 2] = jnp.where(lane < NY - 1, up_y - half[1], 0.0)
        cof[z, 3] = jnp.where(lane > 0, down_y + half[1], 0.0)
        cof[z, 4] = jnp.where(column < NX - 1, up_x - half[2], 0.0)
        cof[z, 5] = jnp.where(column > 0, down_x + half[2], 0.0)
        for j, (real, other, imag) in enumerate(shifts):
            den = real + diagonal
            scale = 1.0 / (den * den + imag * imag)
            cof[z, 6 + 2 * j] = den * scale
            cof[z, 7 + 2 * j] = -imag * scale
            if j == 0:
                den = other + diagonal
                cof[z, 14] = den / (den * den + imag * imag)


def divide(cof, z, j, total_real, total_imag):
    inv_real, inv_imag = cof[z, 6 + 2 * j], cof[z, 7 + 2 * j]
    inv_other = cof[z, 14] if j == 0 else inv_real
    return (
        total_real * inv_real - total_imag * inv_imag,
        total_real * inv_imag + total_imag * inv_other,
    )


def part_of(field, z, r, ahead=0):
    start = 8 + WIDE * (REALS * z + r) + ahead
    return field.at[start : start + WIDE]


def sweeps(group, cof, spec_of, src, dst, planes, shift, finish):
    for number, (first, end) in enumerate(planes):
        for z in range(first, end):
            here = z + shift
            for j in range(EACH):
                totals = []
                for r in (j, EACH + j):
                    centre = part_of(src, here, r)[...]
                    total = cof[z, 0] * part_of(src, here + 1, r)[...] + cof[z, 1] * part_of(src, here - 1, r)[...]
                    total += cof[z, 2] * pltpu.roll(centre, NY - 1, 1) + cof[z, 3] * pltpu.roll(centre, 1, 1)
                    total += cof[z, 4] * part_of(src, here, r, 1)[...] + cof[z, 5] * part_of(src, here, r, -1)[...]
                    totals.append(total + spec_of(z, r))
                for r, value in zip((j, EACH + j), divide(cof, z, EACH * group + j, *totals)):
                    if number == len(planes) - 1:
                        finish(z, r, value)
                    else:
                        part_of(dst, here, r)[...] = value
        src, dst = dst, src


def spectrum_reader(chip, pair, other):
    def spec_of(z, r):
        if z < FIRST:
            return pick(other[z, r], pair[z, r])
        if z < FIRST + CHIP:
            return chip[z - FIRST, r]
        return pick(pair[z - FIRST - CHIP, r], other[z - FIRST - CHIP, r])

    return spec_of


def first_kernel(group, chip, other, pair, cof, out, field_a, field_b):
    spec_of = spectrum_reader(chip, pair, other)
    for field in (field_a, field_b):
        field[0:8] = jnp.zeros((8, NY), jnp.float32)
        field[8 + WIDE * REALS * REACH :] = jnp.zeros((8, NY), jnp.float32)
    for z in range(REACH):
        for j in range(EACH):
            values = divide(cof, z, EACH * group + j, spec_of(z, j), spec_of(z, EACH + j))
            for r, value in zip((j, EACH + j), values):
                part_of(field_a, z, r)[...] = value

    def finish(z, r, value):
        out[z - FIRST, r] = value[4 : 4 + NARROW]

    sweeps(group, cof, spec_of, field_a, field_b, [(1, 9), (2, 8), (3, 7)], 0, finish)


def second_kernel(group, chip, other, pair, cof, own, other_own, pair_own, mine, theirs, field_a, field_b):
    core = lax.axis_index("space") % 2
    spec_of = spectrum_reader(chip, pair, other)
    for field in (field_a, field_b):
        field[0:8] = jnp.zeros((8, NY), jnp.float32)
        field[8 + WIDE * REALS * 3 * CHIP :] = jnp.zeros((8, NY), jnp.float32)
    edge = jnp.zeros((8, NY), jnp.float32)
    sources = ((other_own, pair_own), (own, own), (pair_own, other_own))
    for third, (even, odd) in enumerate(sources):
        for plane in range(CHIP):
            for r in range(REALS):
                spot = part_of(field_a, CHIP * third + plane, r)
                spot[0:8] = edge
                spot[WIDE - 8 : WIDE] = edge
                spot[4 : 4 + NARROW] = own[plane, r] if third == 1 else pick(even[plane, r], odd[plane, r])
    held = {}

    def finish(z, r, value):
        plane = z - FIRST
        value = value[8 : 8 + OWN]
        if plane < SLAB:
            held[plane, r] = value
        else:
            low_value = held.pop((plane - SLAB, r))
            mine[plane - SLAB, r] = jnp.where(core == 0, low_value, value)
            theirs[plane - SLAB, r] = jnp.where(core == 0, value, low_value)

    sweeps(group, cof, spec_of, field_a, field_b, [(0, 10), (1, 9), (2, 8), (3, 7)], 1, finish)


INSIDE_MIB = 53.25


def call(kernel, shapes, args, scratch=(), anywhere=False, mib=32):
    vmem = pl.BlockSpec(memory_space=pltpu.VMEM)
    several = isinstance(shapes, list)
    out_shape = [jax.ShapeDtypeStruct(shape, jnp.float32) for shape in (shapes if several else [shapes])]
    return pl.pallas_call(
        kernel,
        out_shape=out_shape if several else out_shape[0],
        in_specs=[pl.BlockSpec(memory_space=pl.ANY) if anywhere else vmem] * len(args),
        out_specs=[vmem] * len(shapes) if several else vmem,
        scratch_shapes=[pltpu.VMEM(dims, jnp.float32) if isinstance(dims, tuple) else dims for dims in scratch],
        compiler_params=pltpu.CompilerParams(vmem_limit_bytes=int(mib * 1024 * 1024)),
    )(*args)


def shards(forcing, iterate, kappa, velocity):
    block = (SLAB, NY, NX)
    cores = [(i, i ^ 1) for i in range(2 * CHIPS)]
    pairs = [(i, i ^ 2) for i in range(2 * CHIPS)]
    others = [(i, i + 2) for i in range(2 * CHIPS - 2) if i // 2 % 2]
    others += [(j, i) for i, j in others]
    others += [(i, i ^ 1) for i in (0, 1, 2 * CHIPS - 2, 2 * CHIPS - 1)]
    facing = [(i, (i + 1) % (2 * CHIPS)) for i in range(1, 2 * CHIPS, 2)]
    facing += [(j, i) for i, j in facing]
    first, second, outer, inner, fields = call(
        entry_kernel,
        [(NY, NX), (NY, NX), block, block, (4, SLAB, WIDE, NY)],
        (iterate, kappa, velocity),
        [(4, *block), (8, NX + 16, NY), pltpu.SemaphoreType.DMA((10,))],
        anywhere=True,
        mib=53,
    )
    first = lax.ppermute(first, "tm", [(i, (i + 1) % WINDOW) for i in range(WINDOW)])
    second = lax.ppermute(second, "tm", [(i, i // 4 * 4 + (i + 1) % 4) for i in range(WINDOW)])
    outer = lax.ppermute(outer, "space", facing)
    inner = lax.ppermute(inner, "space", cores)
    fields, inner = lax.optimization_barrier((fields, inner))
    fields_other = lax.ppermute(fields, "space", others)
    fields_pair = lax.ppermute(fields, "space", pairs)
    base, rim = call(
        inside_kernel,
        [block, block],
        (forcing, iterate, kappa, velocity),
        [(1, *block), (1, *block), block, (3, *block), pltpu.SemaphoreType.DMA((4,))],
        anywhere=True,
        mib=INSIDE_MIB,
    )
    outer, fields_other, fields_pair = lax.optimization_barrier((outer, fields_other, fields_pair))
    sent = call(
        resid_kernel,
        (WINDOW, SLAB * WIDE + EXTRA, NY),
        (base, rim, iterate, first, second, outer, inner),
        [(SLAB + 1, NX + 16, NY)],
    )
    times = lax.all_to_all(sent, "tm", 0, 0)
    parts = call(
        ahead_kernel,
        [(SLAB, REALS, WIDE, NY)] * GROUPS
        + [(SLAB * REALS, WIDE, NY)] * GROUPS,
        (times,),
    )
    got = [lax.ppermute(sent, "space", cores) for sent in parts[GROUPS:]]
    chips, pair_specs, other_specs = [], [], []
    for group in range(GROUPS):
        shape = (FIRST, REALS, WIDE, NY)
        chip, pair, other = call(gather_kernel, [(CHIP, REALS, WIDE, NY), shape, shape], (parts[group], got[group]))
        chips.append(chip)
        other_specs.append(lax.ppermute(other, "space", others))
        pair_specs.append(lax.ppermute(pair, "space", pairs))
    fields, chips[-1] = lax.optimization_barrier((fields, chips[-1]))
    held = call(pack_kernel, (3, 4, SLAB, WIDE, NY), (fields_pair, fields, fields_other))
    held = lax.ppermute(held, "space", cores)
    cof = call(
        prepare_kernel,
        (REACH, 15, WIDE, NY),
        (fields_pair, fields, fields_other, held),
        [(4, 3 * CHIP, WIDE, NY)],
    )
    owns, pair_owns, other_owns = [], [], []
    for group in range(GROUPS):
        own = call(
            functools.partial(first_kernel, group),
            (CHIP, REALS, NARROW, NY),
            (chips[group], other_specs[group], pair_specs[group], cof),
            [(16 + WIDE * REALS * REACH, NY)] * 2,
        )
        owns.append(own)
        other_owns.append(lax.ppermute(own, "space", others))
        pair_owns.append(lax.ppermute(own, "space", pairs))
    mines, theirs = [], []
    for group in range(GROUPS):
        mine, other = call(
            functools.partial(second_kernel, group),
            [(SLAB, REALS, OWN, NY)] * 2,
            (
                *(chips[group], other_specs[group], pair_specs[group], cof),
                *(owns[group], other_owns[group], pair_owns[group]),
            ),
            [(16 + WIDE * REALS * 3 * CHIP, NY)] * 2,
        )
        mines.append(mine)
        theirs.append(lax.ppermute(other, "space", cores))
    correction = call(back_kernel, (WINDOW, SLAB, OWN, NY), (*mines, *theirs))
    correction = lax.all_to_all(correction, "tm", 0, 0)
    return call(update_kernel, (1, SLAB, NY, NX), (correction, iterate))


def solution(mesh):
    in_specs = (
        P("tm", "space", None, None),
        P("tm", "space", None, None),
        P("space", None, None),
        P(None, "space", None, None),
    )
    out_specs = P("tm", "space", None, None)
    return jax.shard_map(shards, mesh=mesh, in_specs=in_specs, out_specs=out_specs, check_vma=False)
```
